128 devices in a mesh: ctx: 16 (over z_hi, y, core), hd: 8 (over z_lo, x).
Axes of the slice: x: 4, y: 4, z: 4 (z_hi: 2, z_lo: 2; z = z_hi * 2 + z_lo), core: 2. Of those that a mesh axis runs over, the one named last changes fastest.
Arguments:
- block_input: bfloat16 [16384, 1024], P(('hd', 'ctx')), may hold values from -6 to 6
- out_grad: bfloat16 [16384, 1024], P(('hd', 'ctx')), may hold values from -6 to 6
- doc_ids: int32 [16384], replicated, may hold values from 0 to 3, as said below
- w_query: bfloat16 [1024, 1024], P('ctx', 'hd'), may hold values from -0.1875 to 0.1875
- w_key: bfloat16 [1024, 512], P('ctx', 'hd'), may hold values from -0.1875 to 0.1875
- w_value: bfloat16 [1024, 512], P('ctx', 'hd'), may hold values from -0.1875 to 0.1875
- w_out: bfloat16 [1024, 1024], P('ctx', 'hd'), may hold values from -0.75 to 0.75
- w_gate: bfloat16 [1024, 4608], P('ctx', 'hd'), may hold values from -0.1875 to 0.1875
- w_up: bfloat16 [1024, 4608], P('ctx', 'hd'), may hold values from -0.1875 to 0.1875
- w_down: bfloat16 [4608, 1024], P('hd', 'ctx'), may hold values from -0.09375 to 0.09375
- norm_gains: bfloat16 [2048], P(('ctx', 'hd')), may hold values from 0.5 to 1.5
- head_gains: bfloat16 [128], P(('ctx', 'hd')), may hold values from 0.099609375 to 1.8984375
Outputs:
- block_output: bfloat16 [16384, 1024], P(('hd', 'ctx'))
- input_grad: float32 [16384, 1024], P(('hd', 'ctx'))
- w_query_grad: float32 [1024, 1024], P('ctx', 'hd')
- w_key_grad: float32 [1024, 512], P('ctx', 'hd')
- w_value_grad: float32 [1024, 512], P('ctx', 'hd')
- w_out_grad: float32 [1024, 1024], P('ctx', 'hd')
- w_gate_grad: float32 [1024, 4608], P('ctx', 'hd')
- w_up_grad: float32 [1024, 4608], P('ctx', 'hd')
- w_down_grad: float32 [4608, 1024], P('hd', 'ctx')
- norm_gains_grad: float32 [2048], P(('ctx', 'hd'))
- head_gains_grad: float32 [128], P(('ctx', 'hd'))
The draws below stay inside these ranges and needn't reach their ends.
Inputs may be any that keep to these rules, and one draw needn't show every extreme that they name: `doc_ids`: document numbers never fall along the tokens; tokens s * 8192 to (s + 1) * 8192 - 1 hold exactly documents 2 s and 2 s + 1, each of 2048 tokens or more.
All inputs are finite; a program needn't handle non-finite values.
Results may differ from the reference program's by a relative error of at most 0.025.
Values may be sent and summed in bfloat16 or wider, within the bound.
No kernel may reach another device: no remote copies, remote signals or barrier semaphores. Data moves between devices by JAX's collectives and lax.ppermute only.
A program may use at most 192 MiB of HBM per device.

```python
import jax
import jax.numpy as jnp
from jax import lax

D = 1024
H = 16
KVH = 8
DH = 64
FF = 4608
TOKENS = 16384
SEQS = 2
LENGTH = 8192


def draw_doc_ids(key, part):
    key = jax.random.fold_in(key, 7)
    token_index = jnp.arange(TOKENS, dtype=jnp.int32)
    sequence = token_index // LENGTH
    offset = token_index % LENGTH
    cuts = jax.random.randint(key, (SEQS,), LENGTH // 4, 3 * LENGTH // 4 + 1, dtype=jnp.int32)
    return (2 * sequence + (offset >= cuts[sequence]).astype(jnp.int32)).astype(jnp.int32)


def block_scale(stream_key, extent, shards, smallest, top_value):
    factor_of, own = 1.0, jax.random.fold_in(stream_key, 6)
    for position, shards_of in shards:
        heights = jnp.exp(jax.random.uniform(jax.random.fold_in(own, position), (shards_of,), jnp.float32, smallest / len(shards), top_value / len(shards)))
        factor_of = factor_of * jnp.repeat(heights, extent[position] // shards_of).reshape([-1 if axis == position else 1 for axis in range(len(extent))])
    return factor_of


def bell_draw(own_key, extent, deviation, limit, shards=(), held_as=jnp.bfloat16):
    values = deviation * jax.random.normal(own_key, extent, jnp.float32)
    if shards:
        values = values * block_scale(own_key, extent, shards, -0.22, 0.18)
    return jnp.clip(values, -limit, limit).astype(held_as)


def setup_inputs(seed: int = 0) -> dict:
    arg_keys = jax.random.split(jax.random.key(seed), 13)
    block_input = bell_draw(arg_keys[0], (TOKENS, D), 1.0, 6.0, ((0, 128),))
    out_grad = bell_draw(arg_keys[1], (TOKENS, D), 1.0, 6.0, ((0, 128),))
    doc_ids = draw_doc_ids(jax.random.fold_in(arg_keys[12], 71), 0)
    w_query = bell_draw(arg_keys[3], (D, H * DH), D ** -0.5, 0.1875, ((0, 16), (1, 8)))
    w_key = bell_draw(arg_keys[4], (D, KVH * DH), D ** -0.5, 0.1875, ((0, 16), (1, 8)))
    w_value = bell_draw(arg_keys[5], (D, KVH * DH), D ** -0.5, 0.1875, ((0, 16), (1, 8)))
    w_out = bell_draw(arg_keys[6], (H * DH, D), (H * DH // 16) ** -0.5, 0.75, ((0, 16), (1, 8)))
    w_gate = bell_draw(arg_keys[7], (D, FF), D ** -0.5, 0.1875, ((0, 16), (1, 8)))
    w_up = bell_draw(arg_keys[8], (D, FF), D ** -0.5, 0.1875, ((0, 16), (1, 8)))
    w_down = bell_draw(arg_keys[9], (FF, D), FF ** -0.5, 0.09375, ((0, 8), (1, 16)))
    norm_gains = jnp.clip(1.0 + 0.1 * jax.random.normal(arg_keys[10], (2 * D,), jnp.float32), 0.5, 1.5).astype(jnp.bfloat16)
    head_gains = jnp.clip(1.0 + 0.18 * jax.random.normal(arg_keys[11], (2 * DH,), jnp.float32), 0.099609375, 1.8984375).astype(jnp.bfloat16)
    return dict(block_input=block_input, out_grad=out_grad, doc_ids=doc_ids, w_query=w_query, w_key=w_key, w_value=w_value, w_out=w_out, w_gate=w_gate, w_up=w_up, w_down=w_down, norm_gains=norm_gains, head_gains=head_gains)


@jax.custom_vjp
def low(v):
    return lax.optimization_barrier(v.astype(jnp.bfloat16)).astype(jnp.float32)

@jax.custom_vjp
def low_back(v):
    return v

def low_keep(v):
    return (low(v), None)

def low_pass(kept, grad):
    return (grad,)

def back_keep(v):
    return (v, None)

def back_low(kept, grad):
    return (low(grad),)
low.defvjp(low_keep, low_pass)
low_back.defvjp(back_keep, back_low)
epsilon = 1e-06
theta = 1000000.0
big_negative = -1e+30

def matmul_high(left, right):
    return jnp.dot(left, right, precision=lax.Precision.HIGHEST, preferred_element_type=jnp.float32)

def norm_rows(values, scales):
    return values * lax.rsqrt(lax.optimization_barrier(jnp.mean(values * values, axis=-1, keepdims=True)) + epsilon) * scales

def rotary_tables(positions, head_size):
    halfway = head_size // 2
    frequency = theta ** (-(jnp.arange(halfway, dtype=jnp.float32) * 2.0 / head_size))
    angles = positions.astype(jnp.float32)[:, None] * frequency[None, :]
    return (jnp.cos(angles), jnp.sin(angles))

def head_rope(raw_value, scales, cosine, sine_table, head_count):
    row_count = raw_value.shape[0]
    head_size = raw_value.shape[1] // head_count
    halfway = head_size // 2
    shaped = norm_rows(raw_value.reshape(row_count, head_count, head_size), scales)
    leading = shaped[..., :halfway]
    trailing = shaped[..., halfway:]
    cos_wide = cosine[:, None, :]
    sin_wide = sine_table[:, None, :]
    turned = jnp.concatenate([leading * cos_wide - trailing * sin_wide, trailing * cos_wide + leading * sin_wide], axis=-1)
    return turned.reshape(row_count, head_count * head_size)

def attend_sequence(packed):
    queries, key_heads, value_heads, seq_ids, seq_index = packed
    length_here = queries.shape[0]
    block_rows = min(512, length_here)
    share = queries.shape[1] // key_heads.shape[1]
    keys_wide = jnp.repeat(key_heads, share, axis=1)
    values_wide = jnp.repeat(value_heads, share, axis=1)
    scale = queries.shape[2] ** (-0.5)

    def one_block(start):
        query_rows = lax.dynamic_slice_in_dim(queries, start, block_rows, 0)
        query_ids = lax.dynamic_slice_in_dim(seq_ids, start, block_rows, 0)
        query_index = lax.dynamic_slice_in_dim(seq_index, start, block_rows, 0)
        scores = jnp.einsum('qhd,khd->hqk', query_rows, keys_wide, precision=lax.Precision.HIGHEST) * scale
        allowed = (query_ids[:, None] == seq_ids[None, :]) & (seq_index[None, :] <= query_index[:, None])
        scores = low_back(jnp.where(allowed[None], scores, big_negative))
        highest = lax.optimization_barrier(jnp.max(scores, axis=-1, keepdims=True))
        log_total = highest + jnp.log(lax.optimization_barrier(jnp.sum(jnp.exp(scores - highest), axis=-1, keepdims=True)))
        weights = low(jnp.exp(scores - log_total))
        return jnp.einsum('hqk,khd->qhd', weights, values_wide, precision=lax.Precision.HIGHEST)
    starts = jnp.arange(length_here // block_rows, dtype=jnp.int32) * block_rows
    blocks = lax.map(jax.checkpoint(one_block), starts)
    return blocks.reshape(length_here, -1)

def layer_forward(block_input, w_query, w_key, w_value, w_out, w_gate, w_up, w_down, norm_gains, head_gains, doc_ids):
    token_index = jnp.arange(TOKENS, dtype=jnp.int32)
    cosine, sine_table = rotary_tables(token_index % LENGTH, DH)
    normed = low(norm_rows(block_input, norm_gains[:D]))
    query_raw = low_back(matmul_high(normed, w_query))
    key_raw = low_back(matmul_high(normed, w_key))
    queries = low(low_back(head_rope(query_raw, head_gains[:DH], cosine, sine_table, H)))
    key_turned = low(low_back(head_rope(key_raw, head_gains[DH:], cosine, sine_table, KVH)))
    values = low(low_back(matmul_high(normed, w_value)))
    packed = (queries.reshape(SEQS, LENGTH, H, DH), key_turned.reshape(SEQS, LENGTH, KVH, DH), values.reshape(SEQS, LENGTH, KVH, DH), doc_ids.reshape(SEQS, LENGTH), token_index.reshape(SEQS, LENGTH))
    mixed_heads = lax.map(attend_sequence, packed).reshape(TOKENS, H * DH)
    mixed_heads = low(low_back(mixed_heads))
    attended = low_back(matmul_high(mixed_heads, w_out))
    residual = block_input + attended
    normed_second = low(norm_rows(residual, norm_gains[D:]))
    gate_value = low_back(matmul_high(normed_second, w_gate))
    up_value = low_back(matmul_high(normed_second, w_up))
    hidden = low(jax.nn.silu(gate_value) * up_value)
    return residual + matmul_high(hidden, w_down)

def reference(block_input, out_grad, doc_ids, w_query, w_key, w_value, w_out, w_gate, w_up, w_down, norm_gains, head_gains):
    floats = tuple((tensor.astype(jnp.float32) for tensor in (block_input, w_query, w_key, w_value, w_out, w_gate, w_up, w_down, norm_gains, head_gains)))

    def forward(*params):
        return layer_forward(*params, doc_ids)
    result, pullback = jax.vjp(forward, *floats)
    gradients = pullback(out_grad.astype(jnp.float32))
    return (result.astype(jnp.bfloat16), gradients[0], gradients[1], gradients[2], gradients[3], gradients[4], gradients[5], gradients[6], gradients[7], gradients[8], gradients[9])
```

```python
import jax
import jax.numpy as jnp
from jax import lax
from jax.experimental import pallas as pl
from jax.experimental.pallas import tpu as pltpu
from jax.sharding import Mesh
from jax.sharding import PartitionSpec as P

D = 1024
H = 16
KVH = 8
DH = 64
FF = 4608

epsilon = 1e-06
theta = 1000000.0
bf16 = jnp.bfloat16
f32 = jnp.float32

AXES = ("zh", "y", "c", "zl", "x")
GROUP = ("c", "x")
BLOCKS = ("zh", "y")
SHARDS = ("zh", "y", "zl")

KB = 512


def contract(left, right, dims):
    return lax.dot_general(left, right, ((dims[0], dims[1]), ((), ())), preferred_element_type=f32)


def dot_nn(left, right):
    return contract(left, right, ((1,), (0,)))


def dot_nt(left, right):
    return contract(left, right, ((1,), (1,)))


def dot_tn(left, right):
    return contract(left, right, ((0,), (0,)))


def lanes(shape):
    return lax.broadcasted_iota(jnp.int32, shape, len(shape) - 1)


def swing(values):
    return pltpu.roll(values, 64, 1)


def head_rows(packed, upper):
    low = lanes(packed.shape) < 64
    turned = swing(packed)
    if upper:
        first = jnp.where(low, 0.0, turned)
        second = jnp.where(low, 0.0, packed)
    else:
        first = jnp.where(low, packed, 0.0)
        second = jnp.where(low, turned, 0.0)
    return jnp.concatenate([first, second], axis=0)


def key_block(ref, j):
    return ref[pl.ds(2 * (j % 4), 2), :, j // 4]


def spans(info_ref, x_block):
    start = x_block * 2048 + info_ref[0] * 256
    cut = info_ref[1]
    first_from = jnp.where(start >= cut, cut, 0)
    last_from = jnp.where(start + 255 >= cut, cut, 0)
    low = first_from // KB
    high = start // KB
    middle = jnp.minimum((last_from + KB - 1) // KB, high)
    return start, cut, low, middle, high


def allowed_pairs(start, cut, j, query_dim, shape):
    rows = lax.broadcasted_iota(jnp.int32, shape, query_dim)
    query_at = start + (rows & 255)
    key_at = j * KB + lax.broadcasted_iota(jnp.int32, shape, 1 - query_dim)
    query_from = jnp.where(query_at >= cut, cut, 0)
    return (key_at <= query_at) & (key_at >= query_from)


def with_ones(kv):
    return jnp.where(lanes(kv.shape) < 64, jnp.ones_like(kv), kv)


def attend_kernel(info_ref, q_ref, kv_ref, mixed_ref, low_ref, inverse_ref, acc_ref):
    x_block = pl.program_id(0)
    start, cut, low, middle, high = spans(info_ref, x_block)
    queries = head_rows(q_ref[:, 0].reshape(256, 128).astype(f32), False).astype(bf16)
    acc_ref[...] = jnp.zeros_like(acc_ref)

    def step(masked):
        def body(j, carry):
            kv = key_block(kv_ref, j).reshape(KB, 128)
            weights = jnp.exp(dot_nt(queries, kv))
            if masked:
                allowed = allowed_pairs(start, cut, j, 0, weights.shape)
                weights = jnp.where(allowed, weights, 0.0)
            acc_ref[...] += dot_nn(weights.astype(bf16), with_ones(kv))
            return carry

        return body

    lax.fori_loop(low, middle, step(True), 0)
    lax.fori_loop(middle, high, step(False), 0)
    step(True)(high, 0)
    sums = acc_ref[...]
    turned = swing(sums)
    is_low = lanes((256, 128)) < 64
    first, second = sums[:256], sums[256:]
    first_turned, second_turned = turned[:256], turned[256:]
    inverse = 1.0 / jnp.where(is_low, first, second_turned)
    mixed = jnp.where(is_low, first_turned, second) * inverse
    mixed_ref[...] = mixed.reshape(mixed_ref.shape)
    low_ref[...] = mixed.astype(bf16).reshape(low_ref.shape)
    inverse_ref[...] = inverse.reshape(inverse_ref.shape)


def chunk_spec():
    return pl.BlockSpec((2, 1, 128, 128), lambda i: (0, i, 0, 0))


def whole_spec(shape):
    return pl.BlockSpec(shape, lambda i: (0,) * len(shape))


def attend(info, queries, kv):
    out = jax.ShapeDtypeStruct((2, 4, 128, 128), f32)
    return pl.pallas_call(
        attend_kernel,
        grid=(4,),
        in_specs=[
            pl.BlockSpec(memory_space=pltpu.SMEM),
            chunk_spec(),
            whole_spec((8, 2, 4, 128, 128)),
        ],
        out_specs=[chunk_spec(), chunk_spec(), chunk_spec()],
        out_shape=[out, jax.ShapeDtypeStruct(out.shape, bf16), out],
        scratch_shapes=[pltpu.VMEM((512, 128), f32)],
        compiler_params=pltpu.CompilerParams(vmem_limit_bytes=40 * 2**20),
        cost_estimate=pl.CostEstimate(
            flops=20 * 10**9, bytes_accessed=4 * 2**20, transcendentals=7 * 10**6
        ),
        name="attend",
    )(info, queries, kv)


def attend_back_kernel(
    info_ref, q_ref, kv_ref, mixed_ref, inverse_ref, grad_ref, dq_ref, dkv_ref, sum_ref, dq_acc
):
    x_block = pl.program_id(0)
    start, cut, low, middle, high = spans(info_ref, x_block)

    @pl.when(x_block == 0)
    def _():
        sum_ref[...] = jnp.zeros_like(sum_ref)

    queries = head_rows(q_ref[:, 0].reshape(256, 128).astype(f32), False).astype(bf16)
    grad = grad_ref[:, 0].reshape(256, 128) * inverse_ref[:, 0].reshape(256, 128)
    grad_rows = head_rows(grad, True)
    product = head_rows(grad * mixed_ref[:, 0].reshape(256, 128), True)
    delta = -jnp.sum(product, axis=1, keepdims=True)
    delta_high = delta.astype(bf16).astype(f32)
    lane = lanes(grad_rows.shape)
    extended = jnp.where(
        lane == 0, delta_high, jnp.where(lane == 1, delta - delta_high, grad_rows)
    ).astype(bf16)
    grad_rows = grad_rows.astype(bf16)
    dq_acc[...] = jnp.zeros_like(dq_acc)

    def step(masked):
        def body(j, carry):
            kv = key_block(kv_ref, j).reshape(KB, 128)
            weights = jnp.exp(dot_nt(kv, queries))
            if masked:
                allowed = allowed_pairs(start, cut, j, 1, weights.shape)
                weights = jnp.where(allowed, weights, 0.0)
            slopes = (weights * dot_nt(with_ones(kv), extended)).astype(bf16)
            total = dot_nn(weights.astype(bf16), grad_rows) + dot_nn(slopes, queries)
            here = (pl.ds(2 * (j % 4), 2), slice(None), j // 4)
            sum_ref[here] = sum_ref[here] + total.reshape(2, 2, 128, 128)
            dq_acc[...] += dot_tn(slopes, kv)
            return carry

        return body

    lax.fori_loop(low, middle, step(True), 0)
    lax.fori_loop(middle, high, step(False), 0)
    step(True)(high, 0)
    sums = dq_acc[...]
    first, second_turned = sums[:256], swing(sums)[256:]
    packed = jnp.where(lanes((256, 128)) < 64, first, second_turned) * DH ** (-0.5)
    dq_ref[...] = packed.reshape(dq_ref.shape)

    @pl.when(x_block == 3)
    def _():
        dkv_ref[...] = sum_ref[...].astype(bf16)


def attend_back(info, queries, kv, mixed, inverse, grad):
    every = (8, 2, 4, 128, 128)
    return pl.pallas_call(
        attend_back_kernel,
        grid=(4,),
        in_specs=[
            pl.BlockSpec(memory_space=pltpu.SMEM),
            chunk_spec(),
            whole_spec(every),
            chunk_spec(),
            chunk_spec(),
            chunk_spec(),
        ],
        out_specs=[chunk_spec(), whole_spec(every)],
        out_shape=[
            jax.ShapeDtypeStruct((2, 4, 128, 128), f32),
            jax.ShapeDtypeStruct(every, bf16),
        ],
        scratch_shapes=[pltpu.VMEM(every, f32), pltpu.VMEM((512, 128), f32)],
        compiler_params=pltpu.CompilerParams(vmem_limit_bytes=48 * 2**20),
        cost_estimate=pl.CostEstimate(
            flops=40 * 10**9, bytes_accessed=8 * 2**20, transcendentals=7 * 10**6
        ),
        name="attend_back",
    )(info, queries, kv, mixed, inverse, grad)


def exchange(blocks, axes):
    return lax.all_to_all(blocks, axes, split_axis=0, concat_axis=0, tiled=True)


def gather(shard, axes):
    count = lax.axis_size(axes)
    return exchange(jnp.broadcast_to(shard[None], (count,) + shard.shape), axes)


def scatter_sum(blocks, axes):
    return jnp.sum(exchange(blocks.astype(bf16), axes).astype(f32), axis=0)


def trade(values):
    return lax.ppermute(values, ("c", "zl"), [(0, 0), (1, 2), (2, 1), (3, 3)])


def rotary_tables(positions):
    halfway = DH // 2
    frequency = theta ** (-(jnp.arange(halfway, dtype=f32) * 2.0 / DH))
    angles = positions.astype(f32)[:, None] * frequency[None, :]
    return jnp.cos(angles)[:, None, :], jnp.sin(angles)[:, None, :]


def head_rope(raw, gains, cosine, sine):
    inverse = lax.rsqrt(jnp.mean(raw * raw, axis=-1, keepdims=True) + epsilon)
    shaped = raw * inverse * gains
    leading, trailing = shaped[..., : DH // 2], shaped[..., DH // 2 :]
    return jnp.concatenate(
        [leading * cosine - trailing * sine, trailing * cosine + leading * sine], axis=-1
    )


def norm_back(unit, inverse, gains, grad):
    scaled = grad * gains
    return inverse * (scaled - unit * jnp.mean(unit * scaled, axis=-1, keepdims=True))


def shards(
    block_input,
    out_grad,
    doc_ids,
    w_query,
    w_key,
    w_value,
    w_out,
    w_gate,
    w_up,
    w_down,
    norm_gains,
    head_gains,
):
    zh, y, c, zl, x = (lax.axis_index(name) for name in AXES)
    block = zh * 4 + y
    member = c * 4 + x

    gains = gather(jnp.concatenate([norm_gains, head_gains]), AXES).astype(f32)
    gain_first = gains[:64, :16].reshape(D)
    gain_second = gains[64:, :16].reshape(D)
    head_gain = gains[:, 16].reshape(2, DH)
    wqkv = trade(jnp.concatenate([w_query, w_key, w_value], axis=1))
    wqkv = gather(wqkv, SHARDS).reshape(D, 256)
    inputs = gather(block_input, GROUP).reshape(1024, D)

    wout_part = gather(trade(w_out), SHARDS).reshape(D, 128)
    wout = jnp.transpose(gather(wout_part, GROUP), (1, 0, 2)).reshape(D, D)
    wgate = lax.all_gather(trade(w_gate), SHARDS, axis=0, tiled=True)
    wup = lax.all_gather(trade(w_up), SHARDS, axis=0, tiled=True)
    wdown = lax.all_gather(trade(w_down.T), SHARDS, axis=0, tiled=True)
    out_grads = gather(out_grad, GROUP).reshape(1024, D)

    offsets = jnp.arange(128, dtype=jnp.int32)
    member_x = jnp.arange(4, dtype=jnp.int32)
    member_c = jnp.arange(2, dtype=jnp.int32)
    positions = (
        member_x[None, :, None] * 2048
        + block * 256
        + member_c[:, None, None] * 128
        + offsets[None, None, :]
    ).reshape(1024)
    cosine, sine = rotary_tables(positions)
    inputs = inputs.astype(f32)
    inverse_first = lax.rsqrt(jnp.mean(inputs * inputs, axis=-1, keepdims=True) + epsilon)
    unit_first = inputs * inverse_first
    normed = (unit_first * gain_first).astype(bf16)
    qkv = dot_nn(normed, wqkv)
    qk_raw = qkv[:, :192].reshape(1024, 3, DH)
    qk_gains = head_gain[jnp.array([0, 0, 1])]

    def turn(raw, gains_now):
        return head_rope(raw, gains_now, cosine, sine)

    qk = turn(qk_raw, qk_gains).astype(bf16)
    queries = (qk[:, :2].reshape(1024, 128) * DH ** (-0.5)).astype(bf16).reshape(2, 4, 128, 128)
    kv_own = jnp.concatenate([qk[:, 2], qkv[:, 192:].astype(bf16)], axis=1)
    kv = gather(kv_own, BLOCKS).reshape(8, 2, 4, 128, 128)
    tokens = jnp.arange(doc_ids.shape[0], dtype=jnp.int32)
    cut = jnp.sum(((tokens // 8192 == zl) & (doc_ids == 2 * zl)).astype(jnp.int32))
    info = jnp.stack([block, cut]).astype(jnp.int32)
    mixed_f32, mixed_own, inverse_sum = attend(info, queries, kv)

    mixed = gather(mixed_own.reshape(1024, 128), GROUP)
    mixed = jnp.transpose(mixed, (1, 0, 2)).reshape(1024, D)
    residual = inputs + dot_nn(mixed, wout)
    inverse_second = lax.rsqrt(jnp.mean(residual * residual, axis=-1, keepdims=True) + epsilon)
    unit_second = residual * inverse_second
    normed_second = (unit_second * gain_second).astype(bf16)
    gate = dot_nn(normed_second, wgate)
    up = dot_nn(normed_second, wup)
    grad_hidden = dot_nn(out_grads, wdown)
    sig = 1.0 / (1.0 + jnp.exp(-gate))
    silu = gate * sig
    hidden = (silu * up).astype(bf16)
    grad_gate = (grad_hidden * up * sig * (1.0 + gate * (1.0 - sig))).astype(bf16)
    grad_up = (grad_hidden * silu).astype(bf16)
    grad_second = dot_nt(grad_gate, wgate) + dot_nt(grad_up, wup)
    gain_second_grad = jnp.sum(grad_second * unit_second, axis=0)
    part = norm_back(unit_second, inverse_second, gain_second, grad_second).reshape(8, 128, D)
    is_own = (jnp.arange(8, dtype=jnp.int32) == member)[:, None, None]
    part = part + jnp.where(is_own, out_grads.astype(f32).reshape(8, 128, D), 0.0)
    part = part.astype(bf16)
    grad_mixed = dot_nt(part.reshape(1024, D), wout).astype(bf16)
    grad_mixed = jnp.transpose(grad_mixed.reshape(1024, 8, 128), (1, 0, 2))
    grad_mixed = scatter_sum(grad_mixed, GROUP).reshape(2, 4, 128, 128)

    grad_q, grad_kv = attend_back(info, queries, kv, mixed_f32, inverse_sum, grad_mixed)

    ffn = dot_nt(hidden, wdown).astype(bf16).reshape(8, 128, D)
    part, ffn, held = lax.optimization_barrier((part, ffn, grad_mixed[0, 0, :8]))
    grad_residual = scatter_sum(part, GROUP)
    ffn = scatter_sum(ffn, GROUP)
    residual_own = lax.dynamic_index_in_dim(
        residual.reshape(8, 128, D), member, 0, keepdims=False
    )
    block_output_value = (residual_own + ffn).astype(bf16)
    grad_attended = grad_residual.astype(bf16).reshape(128, 8, 128)
    grad_attended = exchange(jnp.transpose(grad_attended, (1, 0, 2)), GROUP).reshape(1024, 128)
    grad_wout = dot_tn(mixed, grad_attended)
    grad_wgate = dot_tn(normed_second, grad_gate)
    grad_wup = dot_tn(normed_second, grad_up)
    grad_wdown = dot_tn(out_grads, hidden)

    def settle(grad):
        return trade(scatter_sum(grad.reshape((16, 64) + grad.shape[1:]), SHARDS))

    grad_wgate = settle(grad_wgate)
    grad_wup = settle(grad_wup)
    grad_wdown = settle(grad_wdown).T
    grad_wout = settle(grad_wout)

    grad_kv = scatter_sum(grad_kv.reshape(8, 1024, 128), BLOCKS)
    turned = jnp.concatenate([grad_q.reshape(1024, 128), grad_kv[:, :DH]], axis=1)
    raw_grad, head_grads = jax.vjp(turn, qk_raw, qk_gains)[1](turned.reshape(1024, 3, DH))
    head_grads = jnp.concatenate([head_grads[0] + head_grads[1], head_grads[2]])
    raw_grad = jnp.concatenate(
        [raw_grad.reshape(1024, 192).astype(bf16), grad_kv[:, DH:].astype(bf16)], axis=1
    )
    grad_normed = dot_nt(raw_grad, wqkv)
    gain_first_grad = jnp.sum(grad_normed * unit_first, axis=0)
    grad_normed = scatter_sum(grad_normed.astype(bf16).reshape(8, 128, D), GROUP)
    grad_wqkv = settle(dot_tn(normed, raw_grad))
    own_input = block_input.astype(f32)
    own_inverse = lax.rsqrt(jnp.mean(own_input * own_input, axis=-1, keepdims=True) + epsilon)
    input_grad = grad_residual + norm_back(
        own_input * own_inverse, own_inverse, gain_first, grad_normed
    )
    gain_grads = jnp.concatenate(
        [
            jnp.concatenate([gain_first_grad, gain_second_grad]).reshape(128, 16),
            head_grads.reshape(128, 1),
        ],
        axis=1,
    )
    gain_grads = jnp.sum(exchange(gain_grads, AXES), axis=0)
    return (
        block_output_value,
        input_grad,
        grad_wqkv[:, :128],
        grad_wqkv[:, 128:192],
        grad_wqkv[:, 192:],
        grad_wout,
        grad_wgate,
        grad_wup,
        grad_wdown,
        gain_grads[:16],
        gain_grads[16:],
    )


def solution(mesh):
    fine = Mesh(mesh.devices.reshape(2, 4, 2, 2, 4), AXES)
    rows = P(("zl", "x", "zh", "y", "c"), None)
    weight = P(("zh", "y", "c"), ("zl", "x"))
    down = P(("zl", "x"), ("zh", "y", "c"))
    return jax.shard_map(
        shards,
        mesh=fine,
        in_specs=(rows, rows, P()) + (weight,) * 6 + (down, P(AXES), P(AXES)),
        out_specs=(rows, rows) + (weight,) * 6 + (down, P(AXES), P(AXES)),
        check_vma=False,
    )
```

```python
import jax
import jax.numpy as jnp
from jax import lax
from jax.experimental import pallas as pl
from jax.experimental.pallas import tpu as pltpu
from jax.sharding import Mesh
from jax.sharding import PartitionSpec as P

D = 1024
H = 16
KVH = 8
DH = 64
FF = 4608

epsilon = 1e-06
theta = 1000000.0
bf16 = jnp.bfloat16
f32 = jnp.float32

AXES = ("zh", "y", "c", "zl", "x")
GROUP = ("c", "x")

KB = 512


def contract(left, right, dims):
    return lax.dot_general(left, right, ((dims[0], dims[1]), ((), ())), preferred_element_type=f32)


def dot_nn(left, right):
    return contract(left, right, ((1,), (0,)))


def dot_nt(left, right):
    return contract(left, right, ((1,), (1,)))


def dot_tn(left, right):
    return contract(left, right, ((0,), (0,)))


def lanes(shape):
    return lax.broadcasted_iota(jnp.int32, shape, len(shape) - 1)


def swing(values):
    return pltpu.roll(values, 64, 1)


def head_rows(packed, upper):
    low = lanes(packed.shape) < 64
    turned = swing(packed)
    if upper:
        first = jnp.where(low, 0.0, turned)
        second = jnp.where(low, 0.0, packed)
    else:
        first = jnp.where(low, packed, 0.0)
        second = jnp.where(low, turned, 0.0)
    return jnp.concatenate([first, second], axis=0)


def key_place(info_ref, j):
    pair = ((j // 2) % 2 ^ info_ref[2]) * 2 + (j % 2 ^ info_ref[3] // 2)
    return (pl.ds(2 * pair, 2), slice(None), j // 4 ^ info_ref[5])


def spans(info_ref, x_block):
    start = x_block * 2048 + info_ref[0] * 256
    cut = info_ref[1]
    first_from = jnp.where(start >= cut, cut, 0)
    last_from = jnp.where(start + 255 >= cut, cut, 0)
    low = first_from // KB
    high = start // KB
    middle = jnp.minimum((last_from + KB - 1) // KB, high)
    return start, cut, low, middle, high


def allowed_pairs(info_ref, start, cut, j, query_dim, shape):
    core = info_ref[4]
    rows = lax.broadcasted_iota(jnp.int32, shape, query_dim)
    query_at = start + ((rows & 255) ^ core * 128)
    columns = lax.broadcasted_iota(jnp.int32, shape, 1 - query_dim)
    key_at = j * KB + (columns ^ (info_ref[3] % 2 * 256 + core * 128))
    query_from = jnp.where(query_at >= cut, cut, 0)
    return (key_at <= query_at) & (key_at >= query_from)


def with_ones(kv):
    return jnp.where(lanes(kv.shape) < 64, jnp.ones_like(kv), kv)


def join_keys(near_ref, far_ref, kv_ref):
    @pl.when(pl.program_id(0) == 0)
    def _():
        kv_ref[:4] = near_ref[...]
        kv_ref[4:] = far_ref[...]


def attend_kernel(
    info_ref, q_ref, near_ref, far_ref, mixed_ref, low_ref, inverse_ref, acc_ref, kv_ref
):
    join_keys(near_ref, far_ref, kv_ref)
    x_block = pl.program_id(0) ^ info_ref[5]
    start, cut, low, middle, high = spans(info_ref, x_block)
    queries = head_rows(q_ref[:, 0].reshape(256, 128).astype(f32), False).astype(bf16)
    acc_ref[...] = jnp.zeros_like(acc_ref)

    def step(masked):
        def body(j, carry):
            kv = kv_ref[key_place(info_ref, j)].reshape(KB, 128)
            weights = jnp.exp(dot_nt(queries, kv))
            if masked:
                allowed = allowed_pairs(info_ref, start, cut, j, 0, weights.shape)
                weights = jnp.where(allowed, weights, 0.0)
            acc_ref[...] += dot_nn(weights.astype(bf16), with_ones(kv))
            return carry

        return body

    lax.fori_loop(low, middle, step(True), 0)
    lax.fori_loop(middle, high, step(False), 0)
    step(True)(high, 0)
    sums = acc_ref[...]
    turned = swing(sums)
    is_low = lanes((256, 128)) < 64
    first, second = sums[:256], sums[256:]
    first_turned, second_turned = turned[:256], turned[256:]
    inverse = 1.0 / jnp.where(is_low, first, second_turned)
    mixed = jnp.where(is_low, first_turned, second) * inverse
    mixed_ref[...] = mixed.reshape(mixed_ref.shape)
    low_ref[...] = mixed.astype(bf16).reshape(low_ref.shape)
    inverse_ref[...] = inverse.reshape(inverse_ref.shape)


def chunk_spec():
    return pl.BlockSpec((2, 1, 128, 128), lambda i: (0, i, 0, 0))


def whole_spec(shape):
    return pl.BlockSpec(shape, lambda i: (0,) * len(shape))


def attend(info, queries, near, far):
    out = jax.ShapeDtypeStruct((2, 4, 128, 128), f32)
    return pl.pallas_call(
        attend_kernel,
        grid=(4,),
        in_specs=[
            pl.BlockSpec(memory_space=pltpu.SMEM),
            chunk_spec(),
            whole_spec((4, 2, 4, 128, 128)),
            whole_spec((4, 2, 4, 128, 128)),
        ],
        out_specs=[chunk_spec(), chunk_spec(), chunk_spec()],
        out_shape=[out, jax.ShapeDtypeStruct(out.shape, bf16), out],
        scratch_shapes=[pltpu.VMEM((512, 128), f32), pltpu.VMEM((8, 2, 4, 128, 128), bf16)],
        compiler_params=pltpu.CompilerParams(vmem_limit_bytes=40 * 2**20),
        cost_estimate=pl.CostEstimate(
            flops=20 * 10**9, bytes_accessed=4 * 2**20, transcendentals=7 * 10**6
        ),
        name="attend",
    )(info, queries, near, far)


def attend_back_kernel(
    info_ref,
    q_ref,
    near_ref,
    far_ref,
    mixed_ref,
    inverse_ref,
    grad_ref,
    dq_ref,
    dkv_ref,
    sum_ref,
    dq_acc,
    kv_ref,
):
    join_keys(near_ref, far_ref, kv_ref)
    x_block = pl.program_id(0) ^ info_ref[5]
    start, cut, low, middle, high = spans(info_ref, x_block)

    @pl.when(pl.program_id(0) == 0)
    def _():
        sum_ref[...] = jnp.zeros_like(sum_ref)

    queries = head_rows(q_ref[:, 0].reshape(256, 128).astype(f32), False).astype(bf16)
    grad = grad_ref[:, 0].reshape(256, 128) * inverse_ref[:, 0].reshape(256, 128)
    grad_rows = head_rows(grad, True)
    product = head_rows(grad * mixed_ref[:, 0].reshape(256, 128), True)
    delta = -jnp.sum(product, axis=1, keepdims=True)
    delta_high = delta.astype(bf16).astype(f32)
    lane = lanes(grad_rows.shape)
    extended = jnp.where(
        lane == 0, delta_high, jnp.where(lane == 1, delta - delta_high, grad_rows)
    ).astype(bf16)
    grad_rows = grad_rows.astype(bf16)
    dq_acc[...] = jnp.zeros_like(dq_acc)

    def step(masked):
        def body(j, carry):
            kv = kv_ref[key_place(info_ref, j)].reshape(KB, 128)
            weights = jnp.exp(dot_nt(kv, queries))
            if masked:
                allowed = allowed_pairs(info_ref, start, cut, j, 1, weights.shape)
                weights = jnp.where(allowed, weights, 0.0)
            slopes = (weights * dot_nt(with_ones(kv), extended)).astype(bf16)
            total = dot_nn(weights.astype(bf16), grad_rows) + dot_nn(slopes, queries)
            here = key_place(info_ref, j)
            sum_ref[here] = sum_ref[here] + total.reshape(2, 2, 128, 128)
            dq_acc[...] += dot_tn(slopes, kv)
            return carry

        return body

    lax.fori_loop(low, middle, step(True), 0)
    lax.fori_loop(middle, high, step(False), 0)
    step(True)(high, 0)
    sums = dq_acc[...]
    first, second_turned = sums[:256], swing(sums)[256:]
    packed = jnp.where(lanes((256, 128)) < 64, first, second_turned) * DH ** (-0.5)
    dq_ref[...] = packed.reshape(dq_ref.shape)

    @pl.when(pl.program_id(0) == 3)
    def _():
        dkv_ref[...] = sum_ref[...].astype(bf16)


def attend_back(info, queries, near, far, mixed, inverse, grad):
    every = (8, 2, 4, 128, 128)
    part = (4, 2, 4, 128, 128)
    return pl.pallas_call(
        attend_back_kernel,
        grid=(4,),
        in_specs=[
            pl.BlockSpec(memory_space=pltpu.SMEM),
            chunk_spec(),
            whole_spec(part),
            whole_spec(part),
            chunk_spec(),
            chunk_spec(),
            chunk_spec(),
        ],
        out_specs=[chunk_spec(), whole_spec(every)],
        out_shape=[
            jax.ShapeDtypeStruct((2, 4, 128, 128), f32),
            jax.ShapeDtypeStruct(every, bf16),
        ],
        scratch_shapes=[
            pltpu.VMEM(every, f32),
            pltpu.VMEM((512, 128), f32),
            pltpu.VMEM(every, bf16),
        ],
        compiler_params=pltpu.CompilerParams(vmem_limit_bytes=48 * 2**20),
        cost_estimate=pl.CostEstimate(
            flops=40 * 10**9, bytes_accessed=8 * 2**20, transcendentals=7 * 10**6
        ),
        name="attend_back",
    )(info, queries, near, far, mixed, inverse, grad)


def near_spec(columns):
    return pl.BlockSpec((2, 128, columns), lambda i: (jnp.minimum(i, 1), 0, 0))


def far_spec(columns):
    return pl.BlockSpec((2, 128, columns), lambda i: (jnp.maximum(i - 2, 0), 0, 0))


def row_spec(columns):
    return pl.BlockSpec((256, columns), lambda i: (i, 0))


def pick_rows(near_ref, far_ref, rows_ref):
    @pl.when(pl.program_id(0) < 2)
    def _():
        rows_ref[...] = near_ref[...].reshape(rows_ref.shape)

    @pl.when(pl.program_id(0) >= 2)
    def _():
        rows_ref[...] = far_ref[...].reshape(rows_ref.shape)


def put_rows(values, near_ref, far_ref):
    @pl.when(pl.program_id(0) < 2)
    def _():
        near_ref[...] = values.reshape(near_ref.shape)

    @pl.when(pl.program_id(0) >= 2)
    def _():
        far_ref[...] = values.reshape(far_ref.shape)


def add_up(ref, values):
    @pl.when(pl.program_id(0) == 0)
    def _():
        ref[...] = values

    @pl.when(pl.program_id(0) > 0)
    def _():
        ref[...] += values


def fold_rows(values):
    return jnp.sum(values.reshape(-1, 8, values.shape[-1]), axis=0)


def unit_rows(values):
    inverse = lax.rsqrt(jnp.mean(values * values, axis=-1, keepdims=True) + epsilon)
    return values * inverse, inverse


def head_means(values):
    low = lanes(values.shape) < 64
    first = jnp.sum(jnp.where(low, values, 0.0), axis=-1, keepdims=True)
    second = jnp.sum(jnp.where(low, 0.0, values), axis=-1, keepdims=True)
    return jnp.where(low, first, second) * (1.0 / DH)


def partner(values):
    is_first = (lanes(values.shape) & 32) == 0
    return jnp.where(is_first, pltpu.roll(values, 96, 1), pltpu.roll(values, 32, 1))


def shard_rows(info_ref, dy, q):
    shard = (info_ref[2] ^ q // 2) * 8 + (info_ref[3] ^ dy) * 2 + (info_ref[6] ^ q % 2)
    return pl.ds(pl.multiple_of(shard * 64, 64), 64)


def front_kernel(
    info_ref,
    w0_ref,
    w1_ref,
    w2_ref,
    w3_ref,
    near_ref,
    far_ref,
    gain_ref,
    head_ref,
    cos_ref,
    sin_ref,
    w_ref,
    wout_ref,
    raw_ref,
    q_ref,
    kv_ref,
    rows_ref,
):
    pick_rows(near_ref, far_ref, rows_ref)

    @pl.when(pl.program_id(0) == 0)
    def _():
        for dy, source in enumerate((w0_ref, w1_ref, w2_ref, w3_ref)):
            for q in range(4):
                w_ref[shard_rows(info_ref, dy, q)] = source[q, :64, :256]
                wout_ref[shard_rows(info_ref, dy, q)] = source[q, :64, 256:]

    unit, inverse = unit_rows(rows_ref[...].astype(f32))
    normed = (unit * gain_ref[...]).astype(bf16)
    raw = dot_nn(normed, w_ref[...])
    raw_ref[...] = raw
    turned = []
    for part in range(2):
        values = raw[:, part * 128 : part * 128 + 128]
        scale = lax.rsqrt(head_means(values * values) + epsilon) * head_ref[part : part + 1]
        shaped = values * scale
        turned.append(shaped * cos_ref[...] + partner(shaped) * sin_ref[...])
    q_ref[...] = (turned[0].astype(bf16).astype(f32) * DH ** (-0.5)).astype(bf16)
    low = lanes(turned[1].shape) < 64
    kv_ref[...] = jnp.where(low, turned[1], raw[:, 128:]).astype(bf16)


def front(info, wqkv, near, far, gain, head_gain, cosine, sine):
    return pl.pallas_call(
        front_kernel,
        grid=(4,),
        in_specs=[pl.BlockSpec(memory_space=pltpu.SMEM)]
        + [whole_spec(wqkv[0].shape)] * 4
        + [
            near_spec(D),
            far_spec(D),
            whole_spec((1, D)),
            whole_spec((2, 128)),
            row_spec(128),
            row_spec(128),
        ],
        out_specs=[
            whole_spec((D, 256)),
            whole_spec((D, 128)),
            row_spec(256),
            row_spec(128),
            row_spec(128),
        ],
        out_shape=[
            jax.ShapeDtypeStruct((D, 256), bf16),
            jax.ShapeDtypeStruct((D, 128), bf16),
            jax.ShapeDtypeStruct((1024, 256), f32),
            jax.ShapeDtypeStruct((1024, 128), bf16),
            jax.ShapeDtypeStruct((1024, 128), bf16),
        ],
        scratch_shapes=[pltpu.VMEM((256, D), bf16)],
        compiler_params=pltpu.CompilerParams(vmem_limit_bytes=32 * 2**20),
        cost_estimate=pl.CostEstimate(flops=6 * 10**9, bytes_accessed=6 * 2**20, transcendentals=0),
        name="front",
    )(info, *wqkv, near, far, gain, head_gain, cosine, sine)


def back_kernel(
    info_ref,
    near_ref,
    far_ref,
    w_ref,
    gain_ref,
    head_ref,
    cos_ref,
    sin_ref,
    raw_ref,
    grad_q_ref,
    grad_kv_ref,
    near_out_ref,
    far_out_ref,
    grad_w_ref,
    gain_grad_ref,
    head_grad_ref,
    rows_ref,
    sum_ref,
):
    pick_rows(near_ref, far_ref, rows_ref)
    unit, inverse = unit_rows(rows_ref[...].astype(f32))
    normed = (unit * gain_ref[...]).astype(bf16)
    raw_grads = []
    head_grads = []
    for part, grad in enumerate((grad_q_ref[...], grad_kv_ref[...])):
        values = raw_ref[:, part * 128 : part * 128 + 128]
        inverse_head = lax.rsqrt(head_means(values * values) + epsilon)
        shaped = values * inverse_head
        turned = grad * cos_ref[...] - partner(grad) * sin_ref[...]
        head_grads.append(fold_rows(turned * shaped))
        scaled = turned * head_ref[part : part + 1]
        raw_grads.append(inverse_head * (scaled - shaped * head_means(shaped * scaled)))
    low = lanes(raw_grads[1].shape) < 64
    raw_grads[1] = jnp.where(low, raw_grads[1], grad_kv_ref[...])
    raw_grad = jnp.concatenate([grad.astype(bf16) for grad in raw_grads], axis=1)
    grad_normed = dot_nt(raw_grad, w_ref[...])
    put_rows(grad_normed.astype(bf16), near_out_ref, far_out_ref)
    add_up(gain_grad_ref, fold_rows(grad_normed * unit))
    add_up(head_grad_ref, jnp.concatenate(head_grads, axis=1))
    add_up(sum_ref, dot_tn(normed, raw_grad))

    @pl.when(pl.program_id(0) == 3)
    def _():
        for dy in range(4):
            for q in range(4):
                rows = sum_ref[shard_rows(info_ref, dy, q)]
                grad_w_ref[dy * 4 + q] = rows.astype(bf16)


def back(info, near, far, wqkv, gain, head_gain, cosine, sine, raw, grad_q, grad_kv):
    blocks = jax.ShapeDtypeStruct((4, 128, D), bf16)
    return pl.pallas_call(
        back_kernel,
        grid=(4,),
        in_specs=[
            pl.BlockSpec(memory_space=pltpu.SMEM),
            near_spec(D),
            far_spec(D),
            whole_spec(wqkv.shape),
            whole_spec((1, D)),
            whole_spec((2, 128)),
            row_spec(128),
            row_spec(128),
            row_spec(256),
            row_spec(128),
            row_spec(128),
        ],
        out_specs=[
            near_spec(D),
            far_spec(D),
            whole_spec((16, 64, 256)),
            whole_spec((8, D)),
            whole_spec((8, 256)),
        ],
        out_shape=[
            blocks,
            blocks,
            jax.ShapeDtypeStruct((16, 64, 256), bf16),
            jax.ShapeDtypeStruct((8, D), f32),
            jax.ShapeDtypeStruct((8, 256), f32),
        ],
        scratch_shapes=[pltpu.VMEM((256, D), bf16), pltpu.VMEM((D, 256), f32)],
        compiler_params=pltpu.CompilerParams(vmem_limit_bytes=40 * 2**20),
        cost_estimate=pl.CostEstimate(flops=8 * 10**9, bytes_accessed=9 * 2**20, transcendentals=0),
        name="back",
    )(info, near, far, wqkv, gain, head_gain, cosine, sine, raw, grad_q, grad_kv)


def middle_kernel(
    info_ref,
    mixed_near_ref,
    mixed_far_ref,
    near_ref,
    far_ref,
    grad_near_ref,
    grad_far_ref,
    wout_near_ref,
    wout_far_ref,
    w0_ref,
    w1_ref,
    w2_ref,
    w3_ref,
    gain_ref,
    mixed_ref,
    own_ref,
    normed_ref,
    hidden_ref,
    grad_gate_ref,
    grad_up_ref,
    part_near_ref,
    part_far_ref,
    mixed_grad_near_ref,
    mixed_grad_far_ref,
    ffn_near_ref,
    ffn_far_ref,
    gain_grad_ref,
    rows_ref,
    grad_ref,
    wout_ref,
    w_ref,
):
    i = pl.program_id(0)
    pick_rows(near_ref, far_ref, rows_ref)
    pick_rows(grad_near_ref, grad_far_ref, grad_ref)

    @pl.when(i == 0)
    def _():
        member = info_ref[4] * 4 + info_ref[5]
        for k in range(8):
            start = pl.multiple_of((member ^ k) * 128, 128)
            for g in range(8):
                columns = pl.ds(pl.multiple_of((member ^ g) * 128, 128), 128)
                source = wout_near_ref if g < 4 else wout_far_ref
                wout_ref[k * 128 : k * 128 + 128, columns] = source[g % 4, pl.ds(start, 128)]

        for dy, source in enumerate((w0_ref, w1_ref, w2_ref, w3_ref)):
            for q in range(4):
                for n in range(3):
                    w_ref[n, shard_rows(info_ref, dy, q)] = source[q, n * 64 : n * 64 + 64]

    for k in range(8):
        source = mixed_near_ref if k < 4 else mixed_far_ref
        for half in range(2):
            mixed_ref[half * 128 : half * 128 + 128, k * 128 : k * 128 + 128] = source[
                k % 4, (2 * i + half) ^ k
            ]
    wgate, wup, wdown = (w_ref[n] for n in range(3))
    residual = rows_ref[...].astype(f32) + dot_nn(mixed_ref[...], wout_ref[...])
    unit, inverse = unit_rows(residual)
    gain = gain_ref[...]
    normed = (unit * gain).astype(bf16)
    normed_ref[...] = normed
    grad = grad_ref[...]
    gate = dot_nn(normed, wgate)
    up = dot_nn(normed, wup)
    grad_hidden = dot_nn(grad, wdown)
    sig = 1.0 / (1.0 + jnp.exp(-gate))
    silu = gate * sig
    hidden = (silu * up).astype(bf16)
    grad_gate = (grad_hidden * up * sig * (1.0 + gate * (1.0 - sig))).astype(bf16)
    grad_up = (grad_hidden * silu).astype(bf16)
    hidden_ref[...] = hidden
    grad_gate_ref[...] = grad_gate
    grad_up_ref[...] = grad_up
    put_rows(dot_nt(hidden, wdown).astype(bf16), ffn_near_ref, ffn_far_ref)
    grad_second = dot_nt(grad_gate, wgate) + dot_nt(grad_up, wup)
    add_up(gain_grad_ref, fold_rows(grad_second * unit))
    scaled = grad_second * gain
    part = inverse * (scaled - unit * jnp.mean(unit * scaled, axis=-1, keepdims=True))
    own = (i == 0) & (lax.broadcasted_iota(jnp.int32, part.shape, 0) < 128)
    part = (part + jnp.where(own, grad.astype(f32), 0.0)).astype(bf16)
    put_rows(part, part_near_ref, part_far_ref)
    grad_mixed = dot_nt(part, wout_ref[...]).astype(bf16)
    for k in range(8):
        target = mixed_grad_near_ref if k < 4 else mixed_grad_far_ref
        for half in range(2):
            target[k % 4, (2 * i + half) ^ k] = grad_mixed[
                half * 128 : half * 128 + 128, k * 128 : k * 128 + 128
            ]

    @pl.when(i == 0)
    def _():
        own_ref[...] = residual[:128]


def middle(info, mixed_near, mixed_far, near, far, grad_near, grad_far, wout, w_ffn, gain):
    hidden = FF // 8

    def out(columns):
        return jax.ShapeDtypeStruct((1024, columns), bf16)

    pieces = (4, 8, 128, 128)
    blocks = jax.ShapeDtypeStruct((4, 128, D), bf16)
    return pl.pallas_call(
        middle_kernel,
        grid=(4,),
        in_specs=[
            pl.BlockSpec(memory_space=pltpu.SMEM),
            whole_spec(pieces),
            whole_spec(pieces),
            near_spec(D),
            far_spec(D),
            near_spec(D),
            far_spec(D),
            whole_spec((4, D, 128)),
            whole_spec((4, D, 128)),
            *[whole_spec((4, 192, hidden))] * 4,
            whole_spec((1, D)),
        ],
        out_specs=[
            row_spec(D),
            whole_spec((128, D)),
            row_spec(D),
            row_spec(hidden),
            row_spec(hidden),
            row_spec(hidden),
            near_spec(D),
            far_spec(D),
            whole_spec(pieces),
            whole_spec(pieces),
            near_spec(D),
            far_spec(D),
            whole_spec((8, D)),
        ],
        out_shape=[
            out(D),
            jax.ShapeDtypeStruct((128, D), f32),
            out(D),
            out(hidden),
            out(hidden),
            out(hidden),
            blocks,
            blocks,
            jax.ShapeDtypeStruct(pieces, bf16),
            jax.ShapeDtypeStruct(pieces, bf16),
            blocks,
            blocks,
            jax.ShapeDtypeStruct((8, D), f32),
        ],
        scratch_shapes=[
            pltpu.VMEM((256, D), bf16),
            pltpu.VMEM((256, D), bf16),
            pltpu.VMEM((D, D), bf16),
            pltpu.VMEM((3, D, hidden), bf16),
        ],
        compiler_params=pltpu.CompilerParams(vmem_limit_bytes=58 * 2**20),
        cost_estimate=pl.CostEstimate(
            flops=20 * 10**9, bytes_accessed=24 * 2**20, transcendentals=10**6
        ),
        name="middle",
    )(info, mixed_near, mixed_far, near, far, grad_near, grad_far, *wout, *w_ffn, gain)


def shard_place(info_ref, shard):
    q = (shard // 8 ^ info_ref[2]) * 2 + (shard % 2 ^ info_ref[6])
    return (shard // 2 % 4 ^ info_ref[3]) * 4 + q


def ffn_grads_kernel(
    info_ref, normed_ref, near_ref, far_ref, hidden_ref, grad_gate_ref, grad_up_ref, out_ref
):
    normed = normed_ref[...]
    grad = jnp.concatenate([near_ref[...].reshape(512, 256), far_ref[...].reshape(512, 256)], axis=0)
    pairs = ((normed, grad_gate_ref), (normed, grad_up_ref), (grad, hidden_ref))
    for n, (left, right_ref) in enumerate(pairs):
        total = dot_tn(left, right_ref[...]).astype(bf16)
        for part in range(4):
            place = shard_place(info_ref, pl.program_id(0) * 4 + part)
            out_ref[place, n * 64 : n * 64 + 64] = total[part * 64 : part * 64 + 64]


def ffn_grads(info, normed, near, far, hidden, grad_gate, grad_up):
    units = FF // 8
    columns = pl.BlockSpec((4, 128, 256), lambda i: (0, 0, i))
    return pl.pallas_call(
        ffn_grads_kernel,
        grid=(4,),
        in_specs=[
            pl.BlockSpec(memory_space=pltpu.SMEM),
            pl.BlockSpec((1024, 256), lambda i: (0, i)),
            columns,
            columns,
        ]
        + [whole_spec((1024, units))] * 3,
        out_specs=whole_spec((16, 192, units)),
        out_shape=jax.ShapeDtypeStruct((16, 192, units), bf16),
        compiler_params=pltpu.CompilerParams(vmem_limit_bytes=40 * 2**20),
        cost_estimate=pl.CostEstimate(
            flops=4 * 10**9, bytes_accessed=12 * 2**20, transcendentals=0
        ),
        name="ffn_grads",
    )(info, normed, near, far, hidden, grad_gate, grad_up)


def out_grads_kernel(info_ref, mixed_ref, grad_ref, out_ref, rows_ref):
    member = info_ref[4] * 4 + info_ref[5]
    for k in range(8):
        rows_ref[k * 128 : k * 128 + 128] = grad_ref[member ^ k]
    for k in range(8):
        total = dot_tn(mixed_ref[:, k * 128 : k * 128 + 128], rows_ref[...])
        for half in range(2):
            place = shard_place(info_ref, (member ^ k) * 2 + half)
            out_ref[place] = total[half * 64 : half * 64 + 64].astype(bf16)


def out_weight_grads(info, mixed, grad):
    return pl.pallas_call(
        out_grads_kernel,
        in_specs=[
            pl.BlockSpec(memory_space=pltpu.SMEM),
            pl.BlockSpec(memory_space=pltpu.VMEM),
            pl.BlockSpec(memory_space=pltpu.VMEM),
        ],
        out_specs=pl.BlockSpec(memory_space=pltpu.VMEM),
        out_shape=jax.ShapeDtypeStruct((16, 64, 128), bf16),
        scratch_shapes=[pltpu.VMEM((1024, 128), bf16)],
        compiler_params=pltpu.CompilerParams(vmem_limit_bytes=32 * 2**20),
        cost_estimate=pl.CostEstimate(flops=10**9, bytes_accessed=3 * 2**20, transcendentals=0),
        name="out_weight_grads",
    )(info, mixed, grad)


def exchange(blocks, axes):
    return lax.all_to_all(blocks, axes, split_axis=0, concat_axis=0, tiled=True)


def swap(values, axis, distance):
    size = lax.axis_size(axis)
    return lax.ppermute(values, axis, [(i, i ^ distance) for i in range(size)])


def ring_near(shard, axis):
    return swap(shard, axis, 1), swap(shard, axis, 3)


def ring_far(shard, near, last, axis):
    half = shard.shape[0] // 2
    far = [swap(last[:half], axis, 1), swap(near[half:], axis, 3)]
    return [shard, near, jnp.concatenate(far, axis=0), last]


def gather_ring(shard, axis):
    near, last = ring_near(shard, axis)
    return ring_far(shard, near, last, axis)


def scatter_far(blocks, axis):
    half = blocks[0].shape[0] // 2
    far_first = swap(blocks[2][:half], axis, 1).astype(f32)
    far_second = swap(blocks[2][half:], axis, 3).astype(f32)
    to_near = jnp.concatenate(
        [blocks[1][:half], (blocks[1][half:].astype(f32) + far_second).astype(bf16)], axis=0
    )
    to_last = jnp.concatenate(
        [(blocks[3][:half].astype(f32) + far_first).astype(bf16), blocks[3][half:]], axis=0
    )
    return blocks[0], to_near, to_last


def scatter_near(own, to_near, to_last, axis):
    total = own.astype(f32) + swap(to_near, axis, 1).astype(f32)
    return total + swap(to_last, axis, 3).astype(f32)


def scatter_ring(blocks, axis):
    return scatter_near(*scatter_far(blocks, axis), axis)


def pair_up(near, far):
    return (near.astype(f32) + swap(far, "c", 1).astype(f32)).astype(bf16)


def scatter_group(near, far):
    paired = pair_up(near, far)
    return scatter_ring([paired[k] for k in range(4)], "x")


def scatter_plain(paired, axis):
    return sum(
        [swap(paired[k], axis, k).astype(f32) for k in (1, 3, 2)], paired[0].astype(f32)
    )


def cross(values, high, core, back):
    pairs = []
    for a in range(2):
        for d in range(2):
            for b in range(2):
                pair = (a * 4 + d * 2 + b, (a ^ high) * 4 + b * 2 + (d ^ core))
                pairs.append(pair[::-1] if back else pair)
    return lax.ppermute(values, ("zh", "c", "zl"), pairs)


def gather_shards(shard):
    return jnp.stack([cross(shard, q // 2, q % 2, False) for q in range(4)])


def scatter_shards(blocks):
    blocks = blocks.astype(bf16)
    return sum(cross(blocks[q], q // 2, q % 2, True).astype(f32) for q in range(4))


def after(values, first):
    return lax.optimization_barrier((values, first))[0]


def rotary_tables(positions):
    lane = jnp.arange(128, dtype=jnp.int32)
    exponents = -(lane % 32).astype(f32) * 2.0 / DH
    angles = positions.astype(f32)[:, None] * (theta**exponents)[None, :]
    sign = jnp.where(lane % 64 < 32, -1.0, 1.0)
    return jnp.cos(angles), jnp.sin(angles) * sign


def shards(
    block_input,
    out_grad,
    doc_ids,
    w_query,
    w_key,
    w_value,
    w_out,
    w_gate,
    w_up,
    w_down,
    norm_gains,
    head_gains,
):
    zh, y, c, zl, x = (lax.axis_index(name) for name in AXES)
    block = zh * 4 + y
    member = c * 4 + x
    tokens = jnp.arange(doc_ids.shape[0], dtype=jnp.int32)
    cut = jnp.sum(((tokens // 8192 == zl) & (doc_ids == 2 * zl)).astype(jnp.int32))

    info = jnp.stack([block, cut, zh, y, c, x, zl]).astype(jnp.int32)
    shard = jnp.concatenate([w_query, w_key, w_value, w_out], axis=1)
    gains = jnp.concatenate([norm_gains, head_gains]).reshape(1, 17)
    shard = jnp.concatenate([shard, jnp.pad(gains, ((0, 15), (0, 367)))], axis=0)
    near = jnp.stack(gather_ring(block_input, "x"))
    wqkv = gather_shards(shard)
    w_ffn = jnp.concatenate([w_gate, w_up, w_down.T], axis=0)
    w_ffn = gather_shards(after(w_ffn, wqkv))
    wqkv = gather_ring(wqkv, "y")
    far = swap(near, "c", 1)
    gains = jnp.stack([part[:, 64, :17] for part in wqkv])
    gains = jnp.stack([gains] + [swap(gains, "x", k) for k in (1, 2, 3)])
    gains = jnp.concatenate([gains, swap(gains, "c", 1)], axis=0).reshape(128, 17)
    slots = jnp.arange(128, dtype=jnp.int32)
    from_high, from_y = zh ^ (slots // 2 % 2), y ^ (slots // 4 % 4)
    from_shard = from_high * 8 + from_y * 2 + (zl ^ (slots % 2))
    holder = from_shard * 8 + (member ^ (slots // 16))
    gains = dot_nn((slots[:, None] == holder[None, :]).astype(bf16), gains)
    gain_first = gains[:64, :16].reshape(1, D)
    gain_second = gains[64:, :16].reshape(1, D)
    head_gain = gains[:, 16].reshape(2, DH)
    head_gain = jnp.concatenate([head_gain, head_gain], axis=1)
    near, w_ffn = lax.optimization_barrier((near, after(w_ffn, wqkv[2])))
    w_ffn_near, w_ffn_last = ring_near(w_ffn, "y")

    offsets = jnp.arange(128, dtype=jnp.int32)
    member_x = jnp.arange(4, dtype=jnp.int32) ^ x
    member_c = jnp.arange(2, dtype=jnp.int32) ^ c
    positions = (
        member_x[None, :, None] * 2048
        + block * 256
        + member_c[:, None, None] * 128
        + offsets[None, None, :]
    ).reshape(1024)
    cosine, sine = rotary_tables(positions)
    wqkv, wout, raw, queries, kv_own = front(
        info, wqkv, near, far, gain_first, head_gain, cosine, sine
    )
    queries = queries.reshape(2, 4, 128, 128)
    kv_other = swap(kv_own, "zh", 1)
    kv_ring = ring_near(kv_own, "y")
    other_ring = ring_near(kv_other, "y")
    kv_ring, w_ffn_near, w_ffn_last = lax.optimization_barrier((kv_ring, w_ffn_near, w_ffn_last))
    w_ffn = ring_far(w_ffn, w_ffn_near, w_ffn_last, "y")
    shape = (4, 2, 4, 128, 128)
    kv_near = jnp.stack(ring_far(kv_own, *kv_ring, "y")).reshape(shape)
    kv_far = jnp.stack(ring_far(kv_other, *other_ring, "y")).reshape(shape)

    wout_near = jnp.stack(gather_ring(wout, "x"))
    grad_near = jnp.stack(gather_ring(after(out_grad, near), "x"))
    queries, grad_near, wout_near, w_ffn = lax.optimization_barrier(
        (queries, grad_near, wout_near, w_ffn)
    )
    grad_far = swap(grad_near, "c", 1)
    wout = (wout_near, swap(wout_near, "c", 1))

    mixed_f32, mixed_own, inverse_sum = attend(info, queries, kv_near, kv_far)

    mixed_near = jnp.stack(gather_ring(mixed_own.reshape(1024, 128), "x"))
    mixed_far = swap(mixed_near, "c", 1)
    (
        mixed,
        residual,
        normed_second,
        hidden,
        grad_gate,
        grad_up,
        part_near,
        part_far,
        grad_mixed_near,
        grad_mixed_far,
        ffn_near,
        ffn_far,
        gain_second_grad,
    ) = middle(
        info,
        mixed_near.reshape(4, 8, 128, 128),
        mixed_far.reshape(4, 8, 128, 128),
        near,
        far,
        grad_near,
        grad_far,
        wout,
        w_ffn,
        gain_second,
    )
    grad_mixed = scatter_group(
        grad_mixed_near.reshape(4, 1024, 128), grad_mixed_far.reshape(4, 1024, 128)
    ).reshape(2, 4, 128, 128)

    grad_wffn = ffn_grads(info, normed_second, grad_near, grad_far, hidden, grad_gate, grad_up)
    grad_wffn = grad_wffn.reshape(4, 4, 192, FF // 8)
    grad_wffn = scatter_far([grad_wffn[k] for k in range(4)], "y")
    part = pair_up(part_near, part_far)
    grad_mixed, grad_wffn, part = lax.optimization_barrier((grad_mixed, grad_wffn, part))
    grad_wffn = scatter_near(*grad_wffn, "y")
    grad_residual = scatter_plain(part, "x")

    grad_q, grad_kv = attend_back(
        info, queries, kv_near, kv_far, mixed_f32, inverse_sum, grad_mixed
    )

    grad_kv, grad_residual, grad_wffn = lax.optimization_barrier(
        (grad_kv, grad_residual, grad_wffn)
    )
    grad_kv = grad_kv.reshape(2, 4, 1024, 128)
    grad_kv = scatter_ring([grad_kv[:, k] for k in range(4)], "y")
    grad_wffn = scatter_shards(grad_wffn)
    ffn = scatter_plain(pair_up(after(ffn_near, grad_mixed), after(ffn_far, grad_mixed)), "x")
    grad_attended = grad_residual.astype(bf16).reshape(128, 8, 128)
    grad_attended = exchange(jnp.transpose(grad_attended, (1, 0, 2)), GROUP)
    grad_wout = out_weight_grads(info, mixed, grad_attended)
    grad_kv = grad_kv[0] + swap(grad_kv[1].astype(bf16), "zh", 1).astype(f32)
    grad_kv, grad_wout, ffn, grad_wffn = lax.optimization_barrier(
        (grad_kv, grad_wout, ffn, grad_wffn)
    )
    block_output_value = (residual + ffn).astype(bf16)
    grad_wffn = grad_wffn.reshape(3, 64, FF // 8)

    grad_near, grad_far, grad_wqkv, gain_first_grad, head_grads = back(
        info,
        near,
        far,
        wqkv,
        gain_first,
        head_gain,
        cosine,
        sine,
        raw,
        grad_q.reshape(1024, 128),
        grad_kv,
    )
    gain_grads = jnp.concatenate([gain_first_grad, gain_second_grad], axis=1)
    gain_grads = jnp.sum(gain_grads, axis=0).reshape(16, 8, 16)
    head_grads = jnp.sum(head_grads, axis=0)
    head_grads = jnp.concatenate(
        [head_grads[:DH] + head_grads[DH:128], head_grads[128 : 128 + DH]]
    ).reshape(16, 8, 1)
    gain_grads = jnp.concatenate([gain_grads, head_grads], axis=2).reshape(16, 1, 136)
    gain_high = gain_grads.astype(bf16)
    gain_low = (gain_grads - gain_high.astype(f32)).astype(bf16)
    extra = jnp.concatenate([gain_high, gain_low], axis=1).reshape(16, 272)
    order = (jnp.arange(16, dtype=jnp.int32)[None, :] == from_shard[:16, None]).astype(bf16)
    extra = dot_nn(order, extra).astype(bf16).reshape(16, 2, 136)
    extra = jnp.pad(extra, ((0, 0), (0, 14), (0, 384 - 136)))
    last = jnp.concatenate([grad_wqkv, grad_wout], axis=2)
    last = jnp.concatenate([last, extra], axis=1).reshape(4, 4, 80, 384)
    last = scatter_shards(scatter_ring([last[k] for k in range(4)], "y"))
    gain_grads = (last[64, :136] + last[65, :136]).reshape(8, 17)
    for axis, distance in (("x", 1), ("x", 2), ("zl", 1)):
        gain_grads = gain_grads + swap(gain_grads, axis, distance)
    gain_grads = lax.dynamic_index_in_dim(gain_grads, zl * 4 + x, 0, keepdims=False)
    grad_normed = scatter_group(grad_near, grad_far)
    unit, inverse = unit_rows(block_input.astype(f32))
    scaled = grad_normed * gain_first
    input_grad = grad_residual + inverse * (
        scaled - unit * jnp.mean(unit * scaled, axis=-1, keepdims=True)
    )
    return (
        block_output_value,
        input_grad,
        last[:64, :128],
        last[:64, 128:192],
        last[:64, 192:256],
        last[:64, 256:],
        grad_wffn[0],
        grad_wffn[1],
        grad_wffn[2].T,
        gain_grads[:16],
        gain_grads[16:],
    )


def solution(mesh):
    fine = Mesh(mesh.devices.reshape(2, 4, 2, 2, 4), AXES)
    rows = P(("zl", "x", "zh", "y", "c"), None)
    weight = P(("zh", "y", "c"), ("zl", "x"))
    down = P(("zl", "x"), ("zh", "y", "c"))
    return jax.shard_map(
        shards,
        mesh=fine,
        in_specs=(rows, rows, P()) + (weight,) * 6 + (down, P(AXES), P(AXES)),
        out_specs=(rows, rows) + (weight,) * 6 + (down, P(AXES), P(AXES)),
        check_vma=False,
    )
```

```python
import jax
import jax.numpy as jnp
from jax import lax
from jax.experimental import pallas as pl
from jax.experimental.pallas import tpu as pltpu
from jax.sharding import Mesh
from jax.sharding import PartitionSpec as P

D = 1024
H = 16
KVH = 8
DH = 64
FF = 4608

epsilon = 1e-06
theta = 1000000.0
bf16 = jnp.bfloat16
f32 = jnp.float32

AXES = ("zh", "y", "c", "zl", "x")
GROUP = ("c", "x")
BLOCKS = ("zh", "y")
SHARDS = ("zh", "y", "zl")

KB = 512


def contract(left, right, dims):
    return lax.dot_general(left, right, ((dims[0], dims[1]), ((), ())), preferred_element_type=f32)


def dot_nn(left, right):
    return contract(left, right, ((1,), (0,)))


def dot_nt(left, right):
    return contract(left, right, ((1,), (1,)))


def dot_tn(left, right):
    return contract(left, right, ((0,), (0,)))


def lanes(shape):
    return lax.broadcasted_iota(jnp.int32, shape, len(shape) - 1)


def swing(values):
    return pltpu.roll(values, 64, 1)


def head_rows(packed, upper):
    low = lanes(packed.shape) < 64
    turned = swing(packed)
    if upper:
        first = jnp.where(low, 0.0, turned)
        second = jnp.where(low, 0.0, packed)
    else:
        first = jnp.where(low, packed, 0.0)
        second = jnp.where(low, turned, 0.0)
    return jnp.concatenate([first, second], axis=0)


def key_place(info_ref, j):
    pair = ((j // 2) % 2 ^ info_ref[2]) * 2 + (j % 2 ^ info_ref[3] // 2)
    return (pl.ds(2 * pair, 2), slice(None), j // 4 ^ info_ref[5])


def spans(info_ref, x_block):
    start = x_block * 2048 + info_ref[0] * 256
    cut = info_ref[1]
    first_from = jnp.where(start >= cut, cut, 0)
    last_from = jnp.where(start + 255 >= cut, cut, 0)
    low = first_from // KB
    high = start // KB
    middle = jnp.minimum((last_from + KB - 1) // KB, high)
    return start, cut, low, middle, high


def allowed_pairs(info_ref, start, cut, j, query_dim, shape):
    core = info_ref[4]
    rows = lax.broadcasted_iota(jnp.int32, shape, query_dim)
    query_at = start + ((rows & 255) ^ core * 128)
    columns = lax.broadcasted_iota(jnp.int32, shape, 1 - query_dim)
    key_at = j * KB + (columns ^ (info_ref[3] % 2 * 256 + core * 128))
    query_from = jnp.where(query_at >= cut, cut, 0)
    return (key_at <= query_at) & (key_at >= query_from)


def with_ones(kv):
    return jnp.where(lanes(kv.shape) < 64, jnp.ones_like(kv), kv)


def join_keys(near_ref, far_ref, kv_ref):
    @pl.when(pl.program_id(0) == 0)
    def _():
        kv_ref[:4] = near_ref[...]
        kv_ref[4:] = far_ref[...]


def attend_kernel(
    info_ref, q_ref, near_ref, far_ref, mixed_ref, low_ref, inverse_ref, acc_ref, kv_ref
):
    join_keys(near_ref, far_ref, kv_ref)
    x_block = pl.program_id(0) ^ info_ref[5]
    start, cut, low, middle, high = spans(info_ref, x_block)
    queries = head_rows(q_ref[:, 0].reshape(256, 128).astype(f32), False).astype(bf16)
    acc_ref[...] = jnp.zeros_like(acc_ref)

    def step(masked):
        def body(j, carry):
            kv = kv_ref[key_place(info_ref, j)].reshape(KB, 128)
            weights = jnp.exp(dot_nt(queries, kv))
            if masked:
                allowed = allowed_pairs(info_ref, start, cut, j, 0, weights.shape)
                weights = jnp.where(allowed, weights, 0.0)
            acc_ref[...] += dot_nn(weights.astype(bf16), with_ones(kv))
            return carry

        return body

    lax.fori_loop(low, middle, step(True), 0)
    lax.fori_loop(middle, high, step(False), 0)
    step(True)(high, 0)
    sums = acc_ref[...]
    turned = swing(sums)
    is_low = lanes((256, 128)) < 64
    first, second = sums[:256], sums[256:]
    first_turned, second_turned = turned[:256], turned[256:]
    inverse = 1.0 / jnp.where(is_low, first, second_turned)
    mixed = jnp.where(is_low, first_turned, second) * inverse
    mixed_ref[...] = mixed.reshape(mixed_ref.shape)
    low_ref[...] = mixed.astype(bf16).reshape(low_ref.shape)
    inverse_ref[...] = inverse.reshape(inverse_ref.shape)


def chunk_spec():
    return pl.BlockSpec((2, 1, 128, 128), lambda i: (0, i, 0, 0))


def whole_spec(shape):
    return pl.BlockSpec(shape, lambda i: (0,) * len(shape))


def attend(info, queries, near, far):
    out = jax.ShapeDtypeStruct((2, 4, 128, 128), f32)
    return pl.pallas_call(
        attend_kernel,
        grid=(4,),
        in_specs=[
            pl.BlockSpec(memory_space=pltpu.SMEM),
            chunk_spec(),
            whole_spec((4, 2, 4, 128, 128)),
            whole_spec((4, 2, 4, 128, 128)),
        ],
        out_specs=[chunk_spec(), chunk_spec(), chunk_spec()],
        out_shape=[out, jax.ShapeDtypeStruct(out.shape, bf16), out],
        scratch_shapes=[pltpu.VMEM((512, 128), f32), pltpu.VMEM((8, 2, 4, 128, 128), bf16)],
        compiler_params=pltpu.CompilerParams(vmem_limit_bytes=40 * 2**20),
        cost_estimate=pl.CostEstimate(
            flops=20 * 10**9, bytes_accessed=4 * 2**20, transcendentals=7 * 10**6
        ),
        name="attend",
    )(info, queries, near, far)


def attend_back_kernel(
    info_ref,
    q_ref,
    near_ref,
    far_ref,
    mixed_ref,
    inverse_ref,
    grad_ref,
    dq_ref,
    dkv_ref,
    sum_ref,
    dq_acc,
    kv_ref,
):
    join_keys(near_ref, far_ref, kv_ref)
    x_block = pl.program_id(0) ^ info_ref[5]
    start, cut, low, middle, high = spans(info_ref, x_block)

    @pl.when(pl.program_id(0) == 0)
    def _():
        sum_ref[...] = jnp.zeros_like(sum_ref)

    queries = head_rows(q_ref[:, 0].reshape(256, 128).astype(f32), False).astype(bf16)
    grad = grad_ref[:, 0].reshape(256, 128) * inverse_ref[:, 0].reshape(256, 128)
    grad_rows = head_rows(grad, True)
    product = head_rows(grad * mixed_ref[:, 0].reshape(256, 128), True)
    delta = -jnp.sum(product, axis=1, keepdims=True)
    delta_high = delta.astype(bf16).astype(f32)
    lane = lanes(grad_rows.shape)
    extended = jnp.where(
        lane == 0, delta_high, jnp.where(lane == 1, delta - delta_high, grad_rows)
    ).astype(bf16)
    grad_rows = grad_rows.astype(bf16)
    dq_acc[...] = jnp.zeros_like(dq_acc)

    def step(masked):
        def body(j, carry):
            kv = kv_ref[key_place(info_ref, j)].reshape(KB, 128)
            weights = jnp.exp(dot_nt(kv, queries))
            if masked:
                allowed = allowed_pairs(info_ref, start, cut, j, 1, weights.shape)
                weights = jnp.where(allowed, weights, 0.0)
            slopes = (weights * dot_nt(with_ones(kv), extended)).astype(bf16)
            total = dot_nn(weights.astype(bf16), grad_rows) + dot_nn(slopes, queries)
            here = key_place(info_ref, j)
            sum_ref[here] = sum_ref[here] + total.reshape(2, 2, 128, 128)
            dq_acc[...] += dot_tn(slopes, kv)
            return carry

        return body

    lax.fori_loop(low, middle, step(True), 0)
    lax.fori_loop(middle, high, step(False), 0)
    step(True)(high, 0)
    sums = dq_acc[...]
    first, second_turned = sums[:256], swing(sums)[256:]
    packed = jnp.where(lanes((256, 128)) < 64, first, second_turned) * DH ** (-0.5)
    dq_ref[...] = packed.reshape(dq_ref.shape)

    @pl.when(pl.program_id(0) == 3)
    def _():
        dkv_ref[...] = sum_ref[...].astype(bf16)


def attend_back(info, queries, near, far, mixed, inverse, grad):
    every = (8, 2, 4, 128, 128)
    part = (4, 2, 4, 128, 128)
    return pl.pallas_call(
        attend_back_kernel,
        grid=(4,),
        in_specs=[
            pl.BlockSpec(memory_space=pltpu.SMEM),
            chunk_spec(),
            whole_spec(part),
            whole_spec(part),
            chunk_spec(),
            chunk_spec(),
            chunk_spec(),
        ],
        out_specs=[chunk_spec(), whole_spec(every)],
        out_shape=[
            jax.ShapeDtypeStruct((2, 4, 128, 128), f32),
            jax.ShapeDtypeStruct(every, bf16),
        ],
        scratch_shapes=[
            pltpu.VMEM(every, f32),
            pltpu.VMEM((512, 128), f32),
            pltpu.VMEM(every, bf16),
        ],
        compiler_params=pltpu.CompilerParams(vmem_limit_bytes=48 * 2**20),
        cost_estimate=pl.CostEstimate(
            flops=10**6, bytes_accessed=10**5, transcendentals=7 * 10**6
        ),
        name="attend_back",
    )(info, queries, near, far, mixed, inverse, grad)


def near_spec(columns):
    return pl.BlockSpec((2, 128, columns), lambda i: (jnp.minimum(i, 1), 0, 0))


def far_spec(columns):
    return pl.BlockSpec((2, 128, columns), lambda i: (jnp.maximum(i - 2, 0), 0, 0))


def row_spec(columns):
    return pl.BlockSpec((256, columns), lambda i: (i, 0))


def pick_rows(near_ref, far_ref, rows_ref):
    @pl.when(pl.program_id(0) < 2)
    def _():
        rows_ref[...] = near_ref[...].reshape(rows_ref.shape)

    @pl.when(pl.program_id(0) >= 2)
    def _():
        rows_ref[...] = far_ref[...].reshape(rows_ref.shape)


def put_rows(values, near_ref, far_ref):
    @pl.when(pl.program_id(0) < 2)
    def _():
        near_ref[...] = values.reshape(near_ref.shape)

    @pl.when(pl.program_id(0) >= 2)
    def _():
        far_ref[...] = values.reshape(far_ref.shape)


def add_up(ref, values):
    @pl.when(pl.program_id(0) == 0)
    def _():
        ref[...] = values

    @pl.when(pl.program_id(0) > 0)
    def _():
        ref[...] += values


def fold_rows(values):
    return jnp.sum(values.reshape(-1, 8, values.shape[-1]), axis=0)


def unit_rows(values):
    inverse = lax.rsqrt(jnp.mean(values * values, axis=-1, keepdims=True) + epsilon)
    return values * inverse, inverse


def head_means(values):
    low = lanes(values.shape) < 64
    first = jnp.sum(jnp.where(low, values, 0.0), axis=-1, keepdims=True)
    second = jnp.sum(jnp.where(low, 0.0, values), axis=-1, keepdims=True)
    return jnp.where(low, first, second) * (1.0 / DH)


def partner(values):
    is_first = (lanes(values.shape) & 32) == 0
    return jnp.where(is_first, pltpu.roll(values, 96, 1), pltpu.roll(values, 32, 1))


def shard_rows(info_ref, dy, q):
    shard = (info_ref[2] ^ q // 2) * 8 + (info_ref[3] ^ dy) * 2 + (info_ref[6] ^ q % 2)
    return pl.ds(pl.multiple_of(shard * 64, 64), 64)


def front_kernel(
    info_ref,
    w0_ref,
    w1_ref,
    w2_ref,
    w3_ref,
    near_ref,
    far_ref,
    gain_ref,
    head_ref,
    cos_ref,
    sin_ref,
    w_ref,
    raw_ref,
    q_ref,
    kv_ref,
    rows_ref,
):
    pick_rows(near_ref, far_ref, rows_ref)

    @pl.when(pl.program_id(0) == 0)
    def _():
        for dy, source in enumerate((w0_ref, w1_ref, w2_ref, w3_ref)):
            for q in range(4):
                w_ref[shard_rows(info_ref, dy, q)] = source[q, :64]

    unit, inverse = unit_rows(rows_ref[...].astype(f32))
    normed = (unit * gain_ref[...]).astype(bf16)
    raw = dot_nn(normed, w_ref[...])
    raw_ref[...] = raw
    turned = []
    for part in range(2):
        values = raw[:, part * 128 : part * 128 + 128]
        scale = lax.rsqrt(head_means(values * values) + epsilon) * head_ref[part : part + 1]
        shaped = values * scale
        turned.append(shaped * cos_ref[...] + partner(shaped) * sin_ref[...])
    q_ref[...] = (turned[0].astype(bf16).astype(f32) * DH ** (-0.5)).astype(bf16)
    low = lanes(turned[1].shape) < 64
    kv_ref[...] = jnp.where(low, turned[1], raw[:, 128:]).astype(bf16)


def front(info, wqkv, near, far, gain, head_gain, cosine, sine):
    return pl.pallas_call(
        front_kernel,
        grid=(4,),
        in_specs=[pl.BlockSpec(memory_space=pltpu.SMEM)]
        + [whole_spec(wqkv[0].shape)] * 4
        + [
            near_spec(D),
            far_spec(D),
            whole_spec((1, D)),
            whole_spec((2, 128)),
            row_spec(128),
            row_spec(128),
        ],
        out_specs=[whole_spec((D, 256)), row_spec(256), row_spec(128), row_spec(128)],
        out_shape=[
            jax.ShapeDtypeStruct((D, 256), bf16),
            jax.ShapeDtypeStruct((1024, 256), f32),
            jax.ShapeDtypeStruct((1024, 128), bf16),
            jax.ShapeDtypeStruct((1024, 128), bf16),
        ],
        scratch_shapes=[pltpu.VMEM((256, D), bf16)],
        compiler_params=pltpu.CompilerParams(vmem_limit_bytes=32 * 2**20),
        cost_estimate=pl.CostEstimate(flops=6 * 10**9, bytes_accessed=6 * 2**20, transcendentals=0),
        name="front",
    )(info, *wqkv, near, far, gain, head_gain, cosine, sine)


def back_kernel(
    near_ref,
    far_ref,
    w_ref,
    gain_ref,
    head_ref,
    cos_ref,
    sin_ref,
    raw_ref,
    grad_q_ref,
    grad_kv_ref,
    near_out_ref,
    far_out_ref,
    grad_w_ref,
    gain_grad_ref,
    head_grad_ref,
    rows_ref,
    sum_ref,
):
    pick_rows(near_ref, far_ref, rows_ref)
    unit, inverse = unit_rows(rows_ref[...].astype(f32))
    normed = (unit * gain_ref[...]).astype(bf16)
    raw_grads = []
    head_grads = []
    for part, grad in enumerate((grad_q_ref[...], grad_kv_ref[...])):
        values = raw_ref[:, part * 128 : part * 128 + 128]
        inverse_head = lax.rsqrt(head_means(values * values) + epsilon)
        shaped = values * inverse_head
        turned = grad * cos_ref[...] - partner(grad) * sin_ref[...]
        head_grads.append(fold_rows(turned * shaped))
        scaled = turned * head_ref[part : part + 1]
        raw_grads.append(inverse_head * (scaled - shaped * head_means(shaped * scaled)))
    low = lanes(raw_grads[1].shape) < 64
    raw_grads[1] = jnp.where(low, raw_grads[1], grad_kv_ref[...])
    raw_grad = jnp.concatenate([grad.astype(bf16) for grad in raw_grads], axis=1)
    grad_normed = dot_nt(raw_grad, w_ref[...])
    put_rows(grad_normed.astype(bf16), near_out_ref, far_out_ref)
    add_up(gain_grad_ref, fold_rows(grad_normed * unit))
    add_up(head_grad_ref, jnp.concatenate(head_grads, axis=1))
    add_up(sum_ref, dot_tn(normed, raw_grad))

    @pl.when(pl.program_id(0) == 3)
    def _():
        grad_w_ref[...] = sum_ref[...].astype(bf16).reshape(grad_w_ref.shape)


def back(near, far, wqkv, gain, head_gain, cosine, sine, raw, grad_q, grad_kv):
    blocks = jax.ShapeDtypeStruct((4, 128, D), bf16)
    return pl.pallas_call(
        back_kernel,
        grid=(4,),
        in_specs=[
            near_spec(D),
            far_spec(D),
            whole_spec(wqkv.shape),
            whole_spec((1, D)),
            whole_spec((2, 128)),
            row_spec(128),
            row_spec(128),
            row_spec(256),
            row_spec(128),
            row_spec(128),
        ],
        out_specs=[
            near_spec(D),
            far_spec(D),
            whole_spec((16, 64, 256)),
            whole_spec((8, D)),
            whole_spec((8, 256)),
        ],
        out_shape=[
            blocks,
            blocks,
            jax.ShapeDtypeStruct((16, 64, 256), bf16),
            jax.ShapeDtypeStruct((8, D), f32),
            jax.ShapeDtypeStruct((8, 256), f32),
        ],
        scratch_shapes=[pltpu.VMEM((256, D), bf16), pltpu.VMEM((D, 256), f32)],
        compiler_params=pltpu.CompilerParams(vmem_limit_bytes=40 * 2**20),
        cost_estimate=pl.CostEstimate(flops=8 * 10**9, bytes_accessed=9 * 2**20, transcendentals=0),
        name="back",
    )(near, far, wqkv, gain, head_gain, cosine, sine, raw, grad_q, grad_kv)


def middle_kernel(
    info_ref,
    mixed_near_ref,
    mixed_far_ref,
    near_ref,
    far_ref,
    grad_near_ref,
    grad_far_ref,
    wout_in_ref,
    w0_ref,
    w1_ref,
    w2_ref,
    w3_ref,
    gain_ref,
    mixed_ref,
    own_ref,
    normed_ref,
    hidden_ref,
    grad_gate_ref,
    grad_up_ref,
    part_near_ref,
    part_far_ref,
    mixed_grad_near_ref,
    mixed_grad_far_ref,
    gain_grad_ref,
    rows_ref,
    grad_ref,
    wout_ref,
    w_ref,
):
    i = pl.program_id(0)
    pick_rows(near_ref, far_ref, rows_ref)
    pick_rows(grad_near_ref, grad_far_ref, grad_ref)

    @pl.when(i == 0)
    def _():
        member = info_ref[4] * 4 + info_ref[5]
        for k in range(8):
            start = pl.multiple_of((member ^ k) * 128, 128)
            for g in range(8):
                wout_ref[k * 128 : k * 128 + 128, g * 128 : g * 128 + 128] = wout_in_ref[
                    g, pl.ds(start, 128)
                ]

        for dy, source in enumerate((w0_ref, w1_ref, w2_ref, w3_ref)):
            for q in range(4):
                for n in range(3):
                    w_ref[n, shard_rows(info_ref, dy, q)] = source[q, n * 64 : n * 64 + 64]

    for k in range(8):
        source = mixed_near_ref if k < 4 else mixed_far_ref
        for half in range(2):
            mixed_ref[half * 128 : half * 128 + 128, k * 128 : k * 128 + 128] = source[
                k % 4, (2 * i + half) ^ k
            ]
    wgate, wup, wdown = (w_ref[n] for n in range(3))
    residual = rows_ref[...].astype(f32) + dot_nn(mixed_ref[...], wout_ref[...])
    unit, inverse = unit_rows(residual)
    gain = gain_ref[...]
    normed = (unit * gain).astype(bf16)
    normed_ref[...] = normed
    grad = grad_ref[...]
    gate = dot_nn(normed, wgate)
    up = dot_nn(normed, wup)
    grad_hidden = dot_nn(grad, wdown)
    sig = 1.0 / (1.0 + jnp.exp(-gate))
    silu = gate * sig
    hidden = (silu * up).astype(bf16)
    grad_gate = (grad_hidden * up * sig * (1.0 + gate * (1.0 - sig))).astype(bf16)
    grad_up = (grad_hidden * silu).astype(bf16)
    hidden_ref[...] = hidden
    grad_gate_ref[...] = grad_gate
    grad_up_ref[...] = grad_up
    ffn = dot_nt(hidden, wdown).astype(bf16)
    grad_second = dot_nt(grad_gate, wgate) + dot_nt(grad_up, wup)
    add_up(gain_grad_ref, fold_rows(grad_second * unit))
    scaled = grad_second * gain
    part = inverse * (scaled - unit * jnp.mean(unit * scaled, axis=-1, keepdims=True))
    own = (i == 0) & (lax.broadcasted_iota(jnp.int32, part.shape, 0) < 128)
    part = (part + jnp.where(own, grad.astype(f32), 0.0)).astype(bf16)
    put_rows(jnp.concatenate([part, ffn], axis=1), part_near_ref, part_far_ref)
    grad_mixed = dot_nt(part, wout_ref[...]).astype(bf16)
    for k in range(8):
        target = mixed_grad_near_ref if k < 4 else mixed_grad_far_ref
        for half in range(2):
            target[k % 4, (2 * i + half) ^ k] = grad_mixed[
                half * 128 : half * 128 + 128, k * 128 : k * 128 + 128
            ]

    @pl.when(i == 0)
    def _():
        own_ref[...] = residual[:128]


def middle(info, mixed_near, mixed_far, near, far, grad_near, grad_far, wout, w_ffn, gain):
    hidden = FF // 8

    def out(columns):
        return jax.ShapeDtypeStruct((1024, columns), bf16)

    pieces = (4, 8, 128, 128)
    blocks = jax.ShapeDtypeStruct((4, 128, 2 * D), bf16)
    return pl.pallas_call(
        middle_kernel,
        grid=(4,),
        in_specs=[
            pl.BlockSpec(memory_space=pltpu.SMEM),
            whole_spec(pieces),
            whole_spec(pieces),
            near_spec(D),
            far_spec(D),
            near_spec(D),
            far_spec(D),
            whole_spec((8, D, 128)),
            *[whole_spec((4, 192, hidden))] * 4,
            whole_spec((1, D)),
        ],
        out_specs=[
            row_spec(D),
            whole_spec((128, D)),
            row_spec(D),
            row_spec(hidden),
            row_spec(hidden),
            row_spec(hidden),
            near_spec(2 * D),
            far_spec(2 * D),
            whole_spec(pieces),
            whole_spec(pieces),
            whole_spec((8, D)),
        ],
        out_shape=[
            out(D),
            jax.ShapeDtypeStruct((128, D), f32),
            out(D),
            out(hidden),
            out(hidden),
            out(hidden),
            blocks,
            blocks,
            jax.ShapeDtypeStruct(pieces, bf16),
            jax.ShapeDtypeStruct(pieces, bf16),
            jax.ShapeDtypeStruct((8, D), f32),
        ],
        scratch_shapes=[
            pltpu.VMEM((256, D), bf16),
            pltpu.VMEM((256, D), bf16),
            pltpu.VMEM((D, D), bf16),
            pltpu.VMEM((3, D, hidden), bf16),
        ],
        compiler_params=pltpu.CompilerParams(vmem_limit_bytes=58 * 2**20),
        cost_estimate=pl.CostEstimate(
            flops=20 * 10**9, bytes_accessed=24 * 2**20, transcendentals=10**6
        ),
        name="middle",
    )(info, mixed_near, mixed_far, near, far, grad_near, grad_far, wout, *w_ffn, gain)


def ffn_grads_kernel(
    normed_ref, near_ref, far_ref, hidden_ref, grad_gate_ref, grad_up_ref, out_ref
):
    shape = (4, 64, FF // 8)
    normed = normed_ref[...]
    grad = jnp.concatenate([near_ref[...].reshape(512, 256), far_ref[...].reshape(512, 256)], axis=0)
    out_ref[:, 0] = dot_tn(normed, grad_gate_ref[...]).astype(bf16).reshape(shape)
    out_ref[:, 1] = dot_tn(normed, grad_up_ref[...]).astype(bf16).reshape(shape)
    out_ref[:, 2] = dot_tn(grad, hidden_ref[...]).astype(bf16).reshape(shape)


def ffn_grads(normed, near, far, hidden, grad_gate, grad_up):
    units = FF // 8
    columns = pl.BlockSpec((4, 128, 256), lambda i: (0, 0, i))
    return pl.pallas_call(
        ffn_grads_kernel,
        grid=(4,),
        in_specs=[pl.BlockSpec((1024, 256), lambda i: (0, i)), columns, columns]
        + [whole_spec((1024, units))] * 3,
        out_specs=pl.BlockSpec((4, 3, 64, units), lambda i: (i, 0, 0, 0)),
        out_shape=jax.ShapeDtypeStruct((16, 3, 64, units), bf16),
        compiler_params=pltpu.CompilerParams(vmem_limit_bytes=40 * 2**20),
        cost_estimate=pl.CostEstimate(
            flops=4 * 10**9, bytes_accessed=12 * 2**20, transcendentals=0
        ),
        name="ffn_grads",
    )(normed, near, far, hidden, grad_gate, grad_up)


def out_grads_kernel(info_ref, mixed_ref, grad_ref, out_ref, rows_ref):
    member = info_ref[4] * 4 + info_ref[5]
    for k in range(8):
        rows_ref[k * 128 : k * 128 + 128] = grad_ref[member ^ k]
    for k in range(8):
        total = dot_tn(mixed_ref[:, k * 128 : k * 128 + 128], rows_ref[...])
        out_ref[member ^ k] = total.astype(bf16)


def out_weight_grads(info, mixed, grad):
    return pl.pallas_call(
        out_grads_kernel,
        in_specs=[
            pl.BlockSpec(memory_space=pltpu.SMEM),
            pl.BlockSpec(memory_space=pltpu.VMEM),
            pl.BlockSpec(memory_space=pltpu.VMEM),
        ],
        out_specs=pl.BlockSpec(memory_space=pltpu.VMEM),
        out_shape=jax.ShapeDtypeStruct((8, 128, 128), bf16),
        scratch_shapes=[pltpu.VMEM((1024, 128), bf16)],
        compiler_params=pltpu.CompilerParams(vmem_limit_bytes=32 * 2**20),
        cost_estimate=pl.CostEstimate(flops=10**9, bytes_accessed=3 * 2**20, transcendentals=0),
        name="out_weight_grads",
    )(info, mixed, grad)


def exchange(blocks, axes):
    return lax.all_to_all(blocks, axes, split_axis=0, concat_axis=0, tiled=True)


def gather(shard, axes):
    count = lax.axis_size(axes)
    return exchange(jnp.broadcast_to(shard[None], (count,) + shard.shape), axes)


def swap(values, axis, distance):
    size = lax.axis_size(axis)
    return lax.ppermute(values, axis, [(i, i ^ distance) for i in range(size)])


def ring_near(shard, axis):
    return swap(shard, axis, 1), swap(shard, axis, 3)


def gather_ring(shard, axis):
    return ring_far(shard, *ring_near(shard, axis), axis)


def ring_far(shard, near, last, axis):
    half = shard.shape[0] // 2
    far = [swap(last[:half], axis, 1), swap(near[half:], axis, 3)]
    return [shard, near, jnp.concatenate(far, axis=0), last]


def scatter_ring(blocks, axis):
    half = blocks[0].shape[0] // 2
    far_first = swap(blocks[2][:half], axis, 1).astype(f32)
    far_second = swap(blocks[2][half:], axis, 3).astype(f32)
    to_near = jnp.concatenate(
        [blocks[1][:half], (blocks[1][half:].astype(f32) + far_second).astype(bf16)], axis=0
    )
    to_last = jnp.concatenate(
        [(blocks[3][:half].astype(f32) + far_first).astype(bf16), blocks[3][half:]], axis=0
    )
    total = blocks[0].astype(f32) + swap(to_near, axis, 1).astype(f32)
    return total + swap(to_last, axis, 3).astype(f32)


def pair_up(near, far):
    return (near.astype(f32) + swap(far, "c", 1).astype(f32)).astype(bf16)


def scatter_group(near, far):
    paired = pair_up(near, far)
    return scatter_ring([paired[k] for k in range(4)], "x")


def scatter_plain(paired, axis):
    return sum(
        [swap(paired[k], axis, k).astype(f32) for k in (1, 3, 2)], paired[0].astype(f32)
    )


def cross(values, high, core, back=False):
    pairs = []
    for a in range(2):
        for d in range(2):
            for b in range(2):
                pair = (a * 4 + d * 2 + b, (a ^ high) * 4 + b * 2 + (d ^ core))
                pairs.append(pair[::-1] if back else pair)
    return lax.ppermute(values, ("zh", "c", "zl"), pairs)


def gather_shards(shard):
    return jnp.stack([cross(shard, q // 2, q % 2) for q in range(4)])


def after(values, first):
    return lax.optimization_barrier((values, first))[0]


def trade(values):
    return lax.ppermute(values, ("c", "zl"), [(0, 0), (1, 2), (2, 1), (3, 3)])


def rotary_tables(positions):
    lane = jnp.arange(128, dtype=jnp.int32)
    exponents = -(lane % 32).astype(f32) * 2.0 / DH
    angles = positions.astype(f32)[:, None] * (theta**exponents)[None, :]
    sign = jnp.where(lane % 64 < 32, -1.0, 1.0)
    return jnp.cos(angles), jnp.sin(angles) * sign


def shards(
    block_input,
    out_grad,
    doc_ids,
    w_query,
    w_key,
    w_value,
    w_out,
    w_gate,
    w_up,
    w_down,
    norm_gains,
    head_gains,
):
    zh, y, c, zl, x = (lax.axis_index(name) for name in AXES)
    block = zh * 4 + y
    member = c * 4 + x
    tokens = jnp.arange(doc_ids.shape[0], dtype=jnp.int32)
    cut = jnp.sum(((tokens // 8192 == zl) & (doc_ids == 2 * zl)).astype(jnp.int32))

    info = jnp.stack([block, cut, zh, y, c, x, zl]).astype(jnp.int32)
    shard = jnp.concatenate([w_query, w_key, w_value], axis=1)
    gains = jnp.concatenate([norm_gains, head_gains]).reshape(1, 17)
    shard = jnp.concatenate([shard, jnp.pad(gains, ((0, 15), (0, 239)))], axis=0)
    near = jnp.stack(gather_ring(block_input, "x"))
    wqkv = gather_shards(shard)
    w_ffn = jnp.concatenate([w_gate, w_up, w_down.T], axis=0)
    w_ffn = gather_shards(after(w_ffn, wqkv))
    wqkv = gather_ring(wqkv, "y")
    far = swap(near, "c", 1)
    gains = jnp.stack([part[:, 64, :17] for part in wqkv])
    gains = jnp.stack([gains] + [swap(gains, "x", k) for k in (1, 2, 3)])
    gains = jnp.concatenate([gains, swap(gains, "c", 1)], axis=0).reshape(128, 17)
    slots = jnp.arange(128, dtype=jnp.int32)
    from_high, from_y = zh ^ (slots // 2 % 2), y ^ (slots // 4 % 4)
    from_shard = from_high * 8 + from_y * 2 + (zl ^ (slots % 2))
    holder = from_shard * 8 + (member ^ (slots // 16))
    gains = dot_nn((slots[:, None] == holder[None, :]).astype(bf16), gains)
    gain_first = gains[:64, :16].reshape(1, D)
    gain_second = gains[64:, :16].reshape(1, D)
    head_gain = gains[:, 16].reshape(2, DH)
    head_gain = jnp.concatenate([head_gain, head_gain], axis=1)

    offsets = jnp.arange(128, dtype=jnp.int32)
    member_x = jnp.arange(4, dtype=jnp.int32) ^ x
    member_c = jnp.arange(2, dtype=jnp.int32) ^ c
    positions = (
        member_x[None, :, None] * 2048
        + block * 256
        + member_c[:, None, None] * 128
        + offsets[None, None, :]
    ).reshape(1024)
    cosine, sine = rotary_tables(positions)
    wqkv, raw, queries, kv_own = front(
        info, wqkv, near, far, gain_first, head_gain, cosine, sine
    )
    queries = queries.reshape(2, 4, 128, 128)
    kv_other = swap(kv_own, "zh", 1)
    shape = (4, 2, 4, 128, 128)
    kv_near = jnp.stack(gather_ring(kv_own, "y")).reshape(shape)
    kv_far = jnp.stack(gather_ring(kv_other, "y")).reshape(shape)

    wout = gather(after(trade(w_out), near), SHARDS).reshape(D, 128)
    wout = gather(after(wout, kv_own), GROUP)
    grad_near = jnp.stack(gather_ring(after(out_grad, near), "x"))
    queries, grad_near, w_ffn, kv_near, kv_far = lax.optimization_barrier(
        (queries, grad_near, w_ffn, kv_near, kv_far)
    )
    w_ffn_ring = ring_near(w_ffn, "y")
    grad_far = swap(grad_near, "c", 1)

    mixed_f32, mixed_own, inverse_sum = attend(info, queries, kv_near, kv_far)

    mixed_own = mixed_own.reshape(1024, 128)
    mixed_ring, w_ffn_ring, wout = lax.optimization_barrier(
        (ring_near(mixed_own, "x"), w_ffn_ring, wout)
    )
    w_ffn = ring_far(w_ffn, *w_ffn_ring, "y")
    mixed_near = jnp.stack(ring_far(mixed_own, *mixed_ring, "x"))
    mixed_near, w_ffn = lax.optimization_barrier((mixed_near, w_ffn))
    mixed_far = swap(mixed_near, "c", 1)
    (
        mixed,
        residual,
        normed_second,
        hidden,
        grad_gate,
        grad_up,
        part_near,
        part_far,
        grad_mixed_near,
        grad_mixed_far,
        gain_second_grad,
    ) = middle(
        info,
        mixed_near.reshape(4, 8, 128, 128),
        mixed_far.reshape(4, 8, 128, 128),
        near,
        far,
        grad_near,
        grad_far,
        wout,
        w_ffn,
        gain_second,
    )
    paired = pair_up(
        grad_mixed_near.reshape(4, 1024, 128), grad_mixed_far.reshape(4, 1024, 128)
    )
    grad_wffn = ffn_grads(normed_second, grad_near, grad_far, hidden, grad_gate, grad_up)
    paired, grad_wffn = lax.optimization_barrier((paired, grad_wffn))
    grad_wffn = exchange(grad_wffn.reshape(16, 192, FF // 8), SHARDS)
    grad_mixed = scatter_ring([paired[k] for k in range(4)], "x").reshape(2, 4, 128, 128)
    part = pair_up(part_near, part_far)
    grad_mixed, part = lax.optimization_barrier((grad_mixed, part))
    sent = [swap(part[k], "x", k) for k in (1, 3, 2)]

    grad_q, grad_kv = attend_back(
        info, queries, kv_near, kv_far, mixed_f32, inverse_sum, grad_mixed
    )

    grad_kv, sent, grad_wffn = lax.optimization_barrier((grad_kv, sent, grad_wffn))
    grad_kv = grad_kv.reshape(2, 4, 1024, 128)
    grad_kv = scatter_ring([grad_kv[:, k] for k in range(4)], "y")
    grad_residual = sum([values.astype(f32) for values in sent], part[0].astype(f32))
    block_output_value = (residual + grad_residual[:, D:]).astype(bf16)
    grad_residual = grad_residual[:, :D]
    grad_attended = grad_residual.astype(bf16).reshape(128, 8, 128)
    grad_attended = exchange(jnp.transpose(grad_attended, (1, 0, 2)), GROUP)
    grad_wffn = jnp.sum(grad_wffn.astype(f32), axis=0).astype(bf16)
    grad_kv, grad_wffn = lax.optimization_barrier((grad_kv, grad_wffn))
    grad_wffn = trade(grad_wffn).astype(f32).reshape(3, 64, FF // 8)
    grad_kv_other = swap(grad_kv[1].astype(bf16), "zh", 1).astype(f32)
    grad_wout = out_weight_grads(info, mixed, grad_attended).reshape(16, 64, 128)
    grad_kv = grad_kv[0] + grad_kv_other
    grad_kv, grad_wout = lax.optimization_barrier((grad_kv, grad_wout))

    grad_near, grad_far, grad_wqkv, gain_first_grad, head_grads = back(
        near,
        far,
        wqkv,
        gain_first,
        head_gain,
        cosine,
        sine,
        raw,
        grad_q.reshape(1024, 128),
        grad_kv,
    )
    gain_grads = jnp.concatenate([gain_first_grad, gain_second_grad], axis=1)
    gain_grads = jnp.sum(gain_grads, axis=0).reshape(16, 8, 16)
    head_grads = jnp.sum(head_grads, axis=0)
    head_grads = jnp.concatenate(
        [head_grads[:DH] + head_grads[DH:128], head_grads[128 : 128 + DH]]
    ).reshape(16, 8, 1)
    gain_grads = jnp.concatenate([gain_grads, head_grads], axis=2).reshape(16, 1, 136)
    gain_high = gain_grads.astype(bf16)
    gain_low = (gain_grads - gain_high.astype(f32)).astype(bf16)
    extra = jnp.pad(
        jnp.concatenate([gain_high, gain_low], axis=1), ((0, 0), (0, 14), (0, 256 - 136))
    )
    last = jnp.concatenate([grad_wqkv, extra], axis=1)
    grad_wout = jnp.pad(grad_wout, ((0, 0), (0, 16), (0, 0)))
    last = jnp.concatenate([last, grad_wout], axis=2).reshape(2, 4, 2, 80, 384)
    last = [
        lax.dynamic_index_in_dim(last, y ^ k, 1, keepdims=False).reshape(4, 80, 384)
        for k in range(4)
    ]
    grad_near, grad_far, last = lax.optimization_barrier((grad_near, grad_far, last))
    paired = pair_up(grad_near, grad_far)
    paired, last = lax.optimization_barrier((paired, last))
    last = scatter_plain(last, "y").astype(bf16)
    last = sum(
        cross(
            lax.dynamic_index_in_dim(
                last, (zh ^ q // 2) * 2 + (zl ^ q % 2), 0, keepdims=False
            ),
            q // 2,
            q % 2,
            True,
        ).astype(f32)
        for q in range(4)
    )
    grad_normed = scatter_ring([paired[k] for k in range(4)], "x")
    grad_wqkv = last[:64]
    grad_wout = grad_wqkv[:, 256:]
    gain_grads = (last[64, :136] + last[65, :136]).reshape(8, 17)
    gain_grads = jnp.sum(exchange(gain_grads, ("zl", "x")), axis=0)
    unit, inverse = unit_rows(block_input.astype(f32))
    scaled = grad_normed * gain_first
    input_grad = grad_residual + inverse * (
        scaled - unit * jnp.mean(unit * scaled, axis=-1, keepdims=True)
    )
    return (
        block_output_value,
        input_grad,
        grad_wqkv[:, :128],
        grad_wqkv[:, 128:192],
        grad_wqkv[:, 192:256],
        grad_wout,
        grad_wffn[0],
        grad_wffn[1],
        grad_wffn[2].T,
        gain_grads[:16],
        gain_grads[16:],
    )


def solution(mesh):
    fine = Mesh(mesh.devices.reshape(2, 4, 2, 2, 4), AXES)
    rows = P(("zl", "x", "zh", "y", "c"), None)
    weight = P(("zh", "y", "c"), ("zl", "x"))
    down = P(("zl", "x"), ("zh", "y", "c"))
    return jax.shard_map(
        shards,
        mesh=fine,
        in_specs=(rows, rows, P()) + (weight,) * 6 + (down, P(AXES), P(AXES)),
        out_specs=(rows, rows) + (weight,) * 6 + (down, P(AXES), P(AXES)),
        check_vma=False,
    )
```
